256 devices in a mesh: comp: 64 (over z, x_lo, y), rank: 4 (over x_hi, core).
Axes of the slice: x: 4 (x_hi: 2, x_lo: 2; x = x_hi * 2 + x_lo), y: 4, z: 8, core: 2. Of those that a mesh axis runs over, the one named last changes fastest.
Arguments:
- density: float32 [256, 16384], P('comp'), may hold values from 0.1 to 1
- row_left: float32 [8, 256], replicated, may hold values from -4 to 4
- col_left: float32 [8, 16384], replicated, may hold values from -4 to 4
- row_right: float32 [8, 256], replicated, may hold values from -4 to 4
- col_right: float32 [8, 16384], replicated, may hold values from -4 to 4
Outputs:
- gain: float32 [256, 16384], P(('comp', 'rank'))
The draws below stay inside these ranges and needn't reach their ends.
All inputs are finite; a program needn't handle non-finite values.
Results may differ from the reference program's by a relative error of at most 0.00021.
Values sent between devices are 32-bit elements; how exact they have to be, the bound alone decides.
A program may use at most 192 MiB of HBM per device.

```python
import math
import jax
import jax.numpy as jnp

NB = 16384
R = 8
NA = 256


def shard_levels(rng, extent, pieces, least, high):
    gain = 1.0
    for dim, blocks in pieces:
        heights = jax.random.uniform(jax.random.fold_in(jax.random.fold_in(rng, 6), dim), (blocks,), jnp.float32, least / len(pieces), high / len(pieces))
        gain = gain * jnp.repeat(jnp.exp(heights), extent[dim] // blocks).reshape((-1,) + (1,) * (len(extent) - 1 - dim))
    return gain


def normal_values(own_key, extent, deviation, bound, dtype=jnp.bfloat16):
    drawn = deviation * jax.random.normal(own_key, extent, jnp.float32)
    return jnp.clip(drawn, min=-bound, max=bound).astype(dtype)


def setup_inputs(seed: int = 0) -> dict:
    key_list = jax.random.split(jax.random.key(seed), 6)
    return {
        "density": jnp.clip(jnp.exp(math.log(1.0) - 2.3025851 * jax.random.uniform(key_list[0], (NA, NB), jnp.float32) ** shard_levels(key_list[0], (NA, NB), ((0, 64),), -0.2, 0.2)), 0.1, 1.0),
        "row_left": normal_values(key_list[1], (R, NA), 1.0, 4.0, jnp.float32),
        "col_left": normal_values(key_list[2], (R, NB), 1.0, 4.0, jnp.float32),
        "row_right": normal_values(key_list[3], (R, NA), 1.0, 4.0, jnp.float32),
        "col_right": normal_values(key_list[4], (R, NB), 1.0, 4.0, jnp.float32),
    }


def reference(density, row_left, col_left, row_right, col_right):
    padded_shape = (2 * NA, 2 * NB)
    running_sum = jnp.zeros((NA, NB), jnp.float32)
    for rank_term in range(R):
        left_field = row_left[rank_term][:, None] * density * col_left[rank_term][None, :]
        right_field = row_right[rank_term][:, None] * density * col_right[rank_term][None, :]
        left_spectrum = jnp.fft.rfft2(left_field, s=padded_shape)
        right_spectrum = jnp.fft.rfft2(right_field, s=padded_shape)
        product = jnp.fft.irfft2(left_spectrum * right_spectrum, s=padded_shape)
        running_sum = running_sum + product[:NA, :NB]
    return (running_sum * (0.5 / math.sqrt(NA * NB))).astype(jnp.float32)
```

```python
import functools
import math

import jax
import jax.numpy as jnp
import ml_dtypes
import numpy as np
from jax import lax
from jax.experimental import pallas as pl
from jax.experimental.pallas import tpu as pltpu
from jax.sharding import PartitionSpec as P

MESH = pl.DeviceIdType.MESH
BF16 = jnp.bfloat16
F32 = jnp.float32
SIZE = {"x": 4, "y": 4, "z": 8}


def halves(table):
    table = np.asarray(table, np.float64)
    high = table.astype(ml_dtypes.bfloat16)
    low = (table - high.astype(np.float64)).astype(ml_dtypes.bfloat16)
    return np.stack([high, low])


def phase(numerator, length, sign):
    angle = sign * 2.0 * np.pi * (np.asarray(numerator) % length) / length
    return np.cos(angle), np.sin(angle)


def as_real(cos, sin):
    return np.block([[cos, -sin], [sin, cos]])


def tables():
    k1, t1 = np.arange(256)[:, None], np.arange(128)[None, :]
    k2, s = np.arange(128)[:, None], np.arange(128)[None, :]
    lead = as_real(*phase(k1 * t1, 256, -1))
    twist = np.stack(phase(k1 * s, 32768, -1)).astype(np.float32)
    trail = as_real(*phase(k2 * s, 128, -1)).T
    back_trail = as_real(*phase(k2 * s, 128, 1)).T
    back_lead = as_real(*phase(np.arange(128)[:, None] * np.arange(256)[None, :], 256, 1))
    order = [2 * c + t + 128 * part for c in range(64) for part in (0, 1) for t in (0, 1)]
    back_lead = back_lead[np.array(order)]
    return halves(lead), twist, halves(trail), halves(back_trail), halves(back_lead)


def final_tables(total):
    grid = np.arange(64)
    cos, sin = phase(grid[:, None] * grid[None, :], 64, 1)
    full = as_real(cos, sin)
    order = [4 * sub + q + 64 * part for q in range(4) for part in (0, 1) for sub in range(16)]
    rows = full[np.array(order)]
    scale = 0.5 / (math.sqrt(total) * 256.0 * 32768.0)
    mix = np.zeros((4, 64, 4, 2, 16))
    for q in range(4):
        for c in range(64):
            a = 4 * c + q
            for r in range(4):
                cc, ss = phase(a * (4 * r + 1), 1024, 1)
                mix[q, c, r, 0, c % 16] = cc * scale
                mix[q, c, r, 1, c % 16] = -ss * scale
    return halves(rows), halves(mix.reshape(4, 64, 128))


def split(value):
    high = value.astype(BF16)
    return high, (value - high.astype(F32)).astype(BF16)


def dot3(first, second):
    dot = functools.partial(jnp.dot, preferred_element_type=F32)
    return dot(first[0], second[0]) + (dot(first[0], second[1]) + dot(first[1], second[0]))


def place():
    comp, rank = lax.axis_index("comp"), lax.axis_index("rank")
    return {"z": comp // 8, "y": comp % 4, "x": rank // 2 * 2 + comp // 4 % 2, "core": rank % 2}


def device(at):
    return {"comp": (at["z"] * 2 + at["x"] % 2) * 4 + at["y"], "rank": at["x"] // 2 * 2 + at["core"]}


PARTS = ((("x", "y", "z"), 0, 20), (("y", "z", "x"), 20, 22), (("z", "x", "y"), 42, 22))


def gather_kernel(d_ref, out_ref, local_sem, send_sem, recv_sem):
    me = place()

    def neighbour(axis, offset):
        return device({**me, axis: (me[axis] + offset) % SIZE[axis]})

    local = pltpu.make_async_copy(
        d_ref.at[pl.ds(me["core"] * 64, 64), pl.ds(me["x"] // 2 * 2, 2)],
        out_ref.at[me["z"], me["y"], me["x"]],
        local_sem,
    )
    local.start()
    barrier = pltpu.get_barrier_semaphore()
    peers = [("x", 1), ("x", 2), ("x", 3), ("y", 1), ("y", 2), ("y", 3), ("z", 1), ("z", -1)]
    for axis, offset in peers:
        pl.semaphore_signal(barrier, inc=1, device_id=neighbour(axis, offset), device_id_type=MESH)
    pl.semaphore_wait(barrier, len(peers))
    local.wait()
    started = []

    def send(block, axis, offset):
        i = len(started)
        copy = pltpu.make_async_remote_copy(
            src_ref=block,
            dst_ref=block,
            send_sem=send_sem.at[i],
            recv_sem=recv_sem.at[i],
            device_id=neighbour(axis, offset),
            device_id_type=MESH,
        )
        copy.start()
        started.append(copy)
        return copy

    def view(done, axis, index, low, count, half=None):
        where = []
        for name in ("z", "y", "x"):
            if name == axis:
                where.append(index % SIZE[name])
            elif name in done:
                if half is not None and name == done[-1]:
                    where.append(pl.ds(half * SIZE[name] // 2, SIZE[name] // 2))
                else:
                    where.append(pl.ds(0, SIZE[name]))
            else:
                where.append(me[name])
        return out_ref.at[tuple(where) + (pl.ds(low, count),)]

    def ring(done, axis, low, count):
        steps = SIZE[axis] // 2
        right = left = None
        for step in range(1, steps + 1):
            half = (0, 1) if done and step == steps else (None, None)
            if right is not None:
                right.wait_recv()
            right = send(view(done, axis, me[axis] - (step - 1), low, count, half[0]), axis, 1)
            if left is not None:
                left.wait_recv()
                left = None
            if done or step < steps:
                left = send(view(done, axis, me[axis] + (step - 1), low, count, half[1]), axis, -1)
            yield
        right.wait_recv()
        if left is not None:
            left.wait_recv()

    def direct(axis, low, count):
        copies = [send(view((), axis, me[axis], low, count), axis, o) for o in range(1, SIZE[axis])]
        yield
        for copy in copies:
            copy.wait_recv()

    def part(order, low, count):
        first, second, third = order
        yield from ring((), first, low, count) if first == "z" else direct(first, low, count)
        yield from ring((first,), second, low, count)
        yield from ring((first, second), third, low, count)

    live = [part(*p) for p in PARTS]
    while live:
        for one in list(live):
            if next(one, 0) == 0:
                live.remove(one)
    for copy in started:
        copy.wait_send()


def gather(density):
    return pl.pallas_call(
        gather_kernel,
        out_shape=jax.ShapeDtypeStruct((8, 4, 4, 64, 2, 128), F32),
        in_specs=[pl.BlockSpec(memory_space=pl.ANY)],
        out_specs=pl.BlockSpec(memory_space=pl.ANY),
        scratch_shapes=[
            pltpu.SemaphoreType.DMA,
            pltpu.SemaphoreType.DMA((64,)),
            pltpu.SemaphoreType.DMA((64,)),
        ],
        compiler_params=pltpu.CompilerParams(collective_id=0, has_side_effects=True),
    )(density)


def rows_kernel(core_ref, d_ref, w_ref, left_ref, right_ref, own_ref, other_ref):
    weights = (w_ref[0], w_ref[1])
    source = d_ref.reshape(128 * 16, 128)
    own_rows = own_ref.reshape(32 * 8, 128)
    other_rows = other_ref.reshape(32 * 8, 128)
    for t in range(8):
        x = jnp.concatenate(
            [source[pl.ds(2 * t + p, 128, stride=16), :] for p in (0, 1)], axis=0
        )
        field = dot3(weights, split(x))
        cols = jnp.concatenate(
            [left_ref[:, t * 128 : (t + 1) * 128], right_ref[:, t * 128 : (t + 1) * 128]], axis=0
        )
        field = field * jnp.concatenate([cols] * 4, axis=0)
        own_rows[pl.ds(t, 32, stride=8), :] = field[:32]
        other_rows[pl.ds(t, 32, stride=8), :] = field[32:]


def rows(core, gathered, weights, col_left, col_right):
    out = jax.ShapeDtypeStruct((32, 64, 128), F32)
    return pl.pallas_call(
        rows_kernel,
        out_shape=(out, out),
        grid_spec=pltpu.PrefetchScalarGridSpec(
            num_scalar_prefetch=1,
            grid=(8,),
            in_specs=[
                pl.BlockSpec((128, 16, 128), lambda i, core: (0, i, 0)),
                pl.BlockSpec((2, 64, 256), lambda i, core: (0, 0, 0)),
                pl.BlockSpec((8, 1024), lambda i, core: (0, core[0] * 8 + i)),
                pl.BlockSpec((8, 1024), lambda i, core: (0, core[0] * 8 + i)),
            ],
            out_specs=[pl.BlockSpec((32, 8, 128), lambda i, core: (0, i, 0))] * 2,
        ),
        compiler_params=pltpu.CompilerParams(vmem_limit_bytes=40 << 20),
    )(core, gathered, weights, col_left, col_right)


def columns_kernel(core_ref, own_ref, got_ref, lead_ref, twist_ref, trail_ref, back_trail_ref, back_lead_ref, out_ref, sum_ref):
    step = pl.program_id(0)
    first = core_ref[0] == 0

    def loaded(part, side):
        own, got = own_ref[part, side, 0], got_ref[part, side, 0]
        return jnp.concatenate([jnp.where(first, own, got), jnp.where(first, got, own)], axis=0)

    def table(ref):
        return ref[0], ref[1]

    x = jnp.concatenate(
        [jnp.concatenate([loaded(part, side) for side in (0, 1)], axis=1) for part in (0, 1)], axis=0
    )
    y = dot3(table(lead_ref), split(x))
    spectra = []
    for side in (0, 1):
        real, imag = y[:256, side * 128 : side * 128 + 128], y[256:, side * 128 : side * 128 + 128]
        cos, sin = twist_ref[0], twist_ref[1]
        turned = jnp.concatenate([real * cos - imag * sin, real * sin + imag * cos], axis=1)
        spectra.append(dot3(split(turned), table(trail_ref)))
    left, right = spectra
    lr, li, rr, ri = left[:, :128], left[:, 128:], right[:, :128], right[:, 128:]
    product = jnp.concatenate([lr * rr - li * ri, lr * ri + li * rr], axis=1)

    @pl.when(step == 0)
    def _():
        sum_ref[...] = product

    @pl.when(step > 0)
    def _():
        sum_ref[...] += product

    @pl.when(step == pl.num_programs(0) - 1)
    def _():
        back = dot3(split(sum_ref[...]), table(back_trail_ref))
        real, imag = back[:, :128], back[:, 128:]
        cos, sin = twist_ref[0], twist_ref[1]
        turned = jnp.concatenate([real * cos + imag * sin, imag * cos - real * sin], axis=0)
        out_ref[...] = dot3(table(back_lead_ref), split(turned))


def columns(core, own, got):
    lead, twist, trail, back_trail, back_lead = tables()

    def whole(array):
        return pl.BlockSpec(array.shape, lambda r, core: (0,) * array.ndim)

    constants = (lead, twist, trail, back_trail, back_lead)
    return pl.pallas_call(
        columns_kernel,
        out_shape=jax.ShapeDtypeStruct((256, 128), F32),
        grid_spec=pltpu.PrefetchScalarGridSpec(
            num_scalar_prefetch=1,
            grid=(8,),
            in_specs=[pl.BlockSpec((2, 2, 1, 64, 128), lambda r, core: (0, 0, r, 0, 0))] * 2
            + [whole(c) for c in constants],
            out_specs=pl.BlockSpec((256, 128), lambda r, core: (0, 0)),
            scratch_shapes=[pltpu.VMEM((256, 256), F32)],
        ),
        compiler_params=pltpu.CompilerParams(vmem_limit_bytes=40 << 20),
    )(core, own.reshape(2, 2, 8, 64, 128), got.reshape(2, 2, 8, 64, 128), *(jnp.asarray(c) for c in constants))


def finish_kernel(q_ref, rows_ref, mix_ref, out_ref, got_ref, part_ref, all_ref, line_ref, sems):
    comp, rank = lax.axis_index("comp"), lax.axis_index("rank")

    def peer(offset):
        return {"comp": (comp + offset) % 64, "rank": rank}

    def other(offset):
        return {"comp": comp, "rank": (rank + offset) % 4}

    barrier = pltpu.get_barrier_semaphore()

    def greet(i, carry):
        pl.semaphore_signal(barrier, inc=1, device_id=peer(i), device_id_type=MESH)
        return carry

    lax.fori_loop(1, 64, greet, 0)
    for i in range(1, 4):
        pl.semaphore_signal(barrier, inc=1, device_id=other(i), device_id_type=MESH)
    pl.semaphore_wait(barrier, 66)

    def exchange(source, target, send_sem, recv_sem):
        own = pltpu.make_async_copy(source.at[comp], target.at[comp], recv_sem)
        own.start()

        def send(i, carry):
            to = peer(i)
            pltpu.make_async_remote_copy(
                src_ref=source.at[to["comp"]],
                dst_ref=target.at[comp],
                send_sem=send_sem,
                recv_sem=recv_sem,
                device_id=to,
                device_id_type=MESH,
            ).start()
            return carry

        lax.fori_loop(1, 64, send, 0)
        pltpu.make_async_copy(source, target, recv_sem).wait()
        rest = pl.ds(0, 63)
        pltpu.make_async_copy(source.at[rest], target.at[rest], send_sem).wait()

    exchange(q_ref, got_ref, sems.at[0], sems.at[1])
    x = jnp.concatenate(
        [
            jnp.concatenate([got_ref[:, 2 * part + t, :] for t in (0, 1)], axis=1)
            for part in (0, 1)
        ],
        axis=0,
    )
    part = dot3((rows_ref[0], rows_ref[1]), split(x))
    for q in range(4):
        part_ref[q] = part[32 * q : 32 * q + 32]
    own = pltpu.make_async_copy(part_ref.at[rank], all_ref.at[rank], sems.at[2])
    own.start()
    copies = []
    for i in range(1, 4):
        to = other(i)
        copy = pltpu.make_async_remote_copy(
            src_ref=part_ref.at[to["rank"]],
            dst_ref=all_ref.at[rank],
            send_sem=sems.at[3 + i],
            recv_sem=sems.at[6 + i],
            device_id=to,
            device_id_type=MESH,
        )
        copy.start()
        copies.append(copy)
    own.wait()
    for copy in copies:
        copy.wait()
    lines = dot3((mix_ref[0, rank], mix_ref[1, rank]), split(all_ref[...].reshape(128, 256)))
    for t in (0, 1):
        line_ref[:, t, :] = lines[:, t * 128 : t * 128 + 128]
    exchange(line_ref, out_ref, sems.at[3], sems.at[10])


def finish(q, total):
    rows_table, mix = final_tables(total)
    vmem = pl.BlockSpec(memory_space=pltpu.VMEM)
    return pl.pallas_call(
        finish_kernel,
        out_shape=jax.ShapeDtypeStruct((64, 2, 128), F32),
        in_specs=[vmem] * 3,
        out_specs=vmem,
        scratch_shapes=[
            pltpu.VMEM((64, 4, 128), F32),
            pltpu.VMEM((4, 32, 256), F32),
            pltpu.VMEM((4, 32, 256), F32),
            pltpu.VMEM((64, 2, 128), F32),
            pltpu.SemaphoreType.DMA((11,)),
        ],
        compiler_params=pltpu.CompilerParams(
            collective_id=1, has_side_effects=True, vmem_limit_bytes=40 << 20
        ),
    )(q.reshape(64, 4, 128), jnp.asarray(rows_table), jnp.asarray(mix))


def row_weights(row_left, row_right):
    comp, rank = lax.axis_index("comp"), lax.axis_index("rank")
    first = 4 * comp + rank
    second = 4 * comp + (rank // 2 * 2 + 1 - rank % 2)
    parity = np.arange(2)[:, None]
    chip = np.arange(128)[None, :]
    z, y, x = chip // 16, chip // 4 % 4, chip % 4
    a = (4 * ((z * 2 + x % 2) * 4 + y) + x // 2 * 2 + parity).reshape(-1)
    perm = jnp.asarray(a, jnp.int32)
    both = jnp.concatenate([row_left, row_right], axis=0)
    both = both.reshape(16, 8, 2, 4, 2, 2).transpose(0, 5, 1, 3, 4, 2).reshape(16, 256)
    frequency = jnp.stack([first, second])
    angle = (perm[None, :] * (4 * frequency[:, None] + 1) % 1024).astype(F32) * (-2.0 * math.pi / 1024)
    turn = jnp.stack([jnp.cos(angle), jnp.sin(angle)], axis=1)
    weights = (turn[:, :, None, :] * both[None, None]).reshape(64, 256)
    high = lax.reduce_precision(weights, 8, 7)
    return jnp.stack([high.astype(BF16), (weights - high).astype(BF16)])


def body(density, row_left, col_left, row_right, col_right):
    core = (lax.axis_index("rank") % 2).astype(jnp.int32).reshape(1)
    weights = row_weights(row_left, row_right)
    gathered = gather(density.reshape(4, 128, 128).transpose(1, 0, 2))
    own, other = rows(core, gathered.reshape(128, 128, 128), weights, col_left, col_right)
    got = lax.ppermute(other, "rank", [(0, 1), (1, 0), (2, 3), (3, 2)])
    q = columns(core, own, got)
    return finish(q, 256 * 16384).reshape(1, 16384)


def solution(mesh):
    return jax.shard_map(
        body,
        mesh=mesh,
        in_specs=(P("comp", None), P(), P(), P(), P()),
        out_specs=P(("comp", "rank"), None),
        check_vma=False,
    )
```

```python
import functools
import math

import jax
import jax.numpy as jnp
import ml_dtypes
import numpy as np
from jax import lax
from jax.experimental import pallas as pl
from jax.experimental.pallas import tpu as pltpu
from jax.sharding import PartitionSpec as P

MESH = pl.DeviceIdType.MESH
BF16 = jnp.bfloat16
F32 = jnp.float32
SIZE = {"x": 4, "y": 4, "z": 8}


def halves(table):
    table = np.asarray(table, np.float64)
    high = table.astype(ml_dtypes.bfloat16)
    low = (table - high.astype(np.float64)).astype(ml_dtypes.bfloat16)
    return np.stack([high, low])


def phase(numerator, length, sign):
    angle = sign * 2.0 * np.pi * (np.asarray(numerator) % length) / length
    return np.cos(angle), np.sin(angle)


def as_real(cos, sin):
    return np.block([[cos, -sin], [sin, cos]])


def tables():
    k1, t1 = np.arange(256)[:, None], np.arange(128)[None, :]
    k2, s = np.arange(128)[:, None], np.arange(128)[None, :]
    lead = as_real(*phase(k1 * t1, 256, -1))
    twist = np.stack(phase(k1 * s, 32768, -1)).astype(np.float32)
    trail = as_real(*phase(k2 * s, 128, -1)).T
    back_trail = as_real(*phase(k2 * s, 128, 1)).T
    back_lead = as_real(*phase(np.arange(128)[:, None] * np.arange(256)[None, :], 256, 1))
    order = [2 * c + t + 128 * part for c in range(64) for part in (0, 1) for t in (0, 1)]
    back_lead = back_lead[np.array(order)]
    return halves(lead), twist, halves(trail), halves(back_trail), halves(back_lead)


def final_tables(total):
    grid = np.arange(64)
    cos, sin = phase(grid[:, None] * grid[None, :], 64, 1)
    full = as_real(cos, sin)
    order = [4 * sub + q + 64 * part for q in range(4) for part in (0, 1) for sub in range(16)]
    rows = full[np.array(order)]
    scale = 0.5 / (math.sqrt(total) * 256.0 * 32768.0)
    mix = np.zeros((4, 64, 4, 2, 16))
    for q in range(4):
        for c in range(64):
            a = 4 * c + q
            for r in range(4):
                cc, ss = phase(a * (4 * r + 1), 1024, 1)
                mix[q, c, r, 0, c % 16] = cc * scale
                mix[q, c, r, 1, c % 16] = -ss * scale
    return halves(rows), halves(mix.reshape(4, 64, 128))


def split(value):
    high = value.astype(BF16)
    return high, (value - high.astype(F32)).astype(BF16)


def dot3(first, second):
    dot = functools.partial(jnp.dot, preferred_element_type=F32)
    return dot(first[0], second[0]) + (dot(first[0], second[1]) + dot(first[1], second[0]))


def place():
    comp, rank = lax.axis_index("comp"), lax.axis_index("rank")
    return {"z": comp // 8, "y": comp % 4, "x": rank // 2 * 2 + comp // 4 % 2, "core": rank % 2}


def device(at):
    return {"comp": (at["z"] * 2 + at["x"] % 2) * 4 + at["y"], "rank": at["x"] // 2 * 2 + at["core"]}


def front_kernel(
    d_ref, row_left_ref, row_right_ref, turn_ref, left_ref, right_ref, out_ref,
    lines_ref, dense_ref, weight_ref, field_ref, one_sem, send_sem, recv_sem,
):
    me = place()
    z, y, x, core = me["z"], me["y"], me["x"], me["core"]
    mine = (z * 2 + x % 2, y)

    def at(**changes):
        moved = dict(me)
        for axis, value in changes.items():
            moved[axis] = value % SIZE[axis] if axis in SIZE else value
        return moved

    def group_x(where):
        return where["x"] % 2 * 4 + where["x"] // 2 * 2 + where["core"]

    def group_y(where):
        return where["y"] * 2 + where["core"]

    loads = [
        pltpu.make_async_copy(d_ref.at[:, row], lines_ref.at[row], one_sem.at[0])
        for row in range(4)
    ]
    for load in loads:
        load.start()
    barrier = pltpu.get_barrier_semaphore()
    friends = [at(z=z + o) for o in range(1, 8)]
    friends += [at(z=z + o, x=x + side) for o in range(8) for side in (1, -1)]
    friends += [at(y=y + o) for o in range(1, 4)]
    friends += [at(y=y + o, x=x + side) for o in range(1, 4) for side in (1, -1)]
    friends += [at(x=x + 2)]
    friends += [at(x=x + o, core=1 - core) for o in range(4)]
    friends += [at(y=y + o, core=1 - core) for o in range(1, 4)]
    for friend in friends:
        pl.semaphore_signal(barrier, inc=1, device_id=device(friend), device_id_type=MESH)

    both = jnp.concatenate([row_left_ref[...], row_right_ref[...]], axis=0)
    for region in (0, 1):
        for p in range(8):
            if region == 0:
                owner = at(x=p // 4 + p % 4 // 2 * 2, core=p % 2)
            else:
                owner = at(y=p // 2, core=p % 2)
            owner = device(owner)
            turn = turn_ref[4 * owner["comp"] + owner["rank"]]
            for part in (0, 1):
                high, low = split(both * turn[part : part + 1])
                first = 32 * p + 16 * part
                weight_ref[region, 0, first : first + 16] = high
                weight_ref[region, 1, first : first + 16] = low

    pltpu.make_async_copy(lines_ref, lines_ref, one_sem.at[0]).wait()
    pl.semaphore_wait(barrier, len(friends))

    def slices(region, where):
        index = group_x(where) if region == 0 else 8 + group_y(where)
        return lines_ref.at[:, pl.ds(pl.multiple_of(8 * index, 8), 8)]

    def spread(region, targets):
        pltpu.make_async_copy(
            slices(region, me), dense_ref.at[(region,) + mine], one_sem.at[3 + region]
        ).start()
        for target in targets:
            pltpu.make_async_remote_copy(
                src_ref=slices(region, target),
                dst_ref=dense_ref.at[(region,) + mine],
                send_sem=one_sem.at[1 + region],
                recv_sem=one_sem.at[3 + region],
                device_id=device(target),
                device_id_type=MESH,
            ).start()

    spread(
        1,
        [at(y=y + o) for o in range(1, 4)]
        + [at(y=y + o, x=x - 1 + (y + o) % 4 % 2 * 2) for o in range(4)],
    )
    spread(
        0,
        [at(z=z + o) for o in range(1, 8)]
        + [at(z=z + o, x=x - 1 + (z + o) % 8 % 2 * 2) for o in range(8)],
    )
    started = []

    def send(block, target):
        i = len(started)
        copy = pltpu.make_async_remote_copy(
            src_ref=block,
            dst_ref=block,
            send_sem=send_sem.at[i],
            recv_sem=recv_sem.at[i],
            device_id=device(target),
            device_id_type=MESH,
        )
        copy.start()
        started.append(copy)
        return copy

    def ring(axis, steps, block):
        ahead = {1: [None, None], -1: [None, None]}
        for step in range(1, steps + 1):
            for turn in (0, 1):
                for way in (1, -1):
                    chunk = turn if way == 1 else 1 - turn
                    if ahead[way][chunk] is not None:
                        ahead[way][chunk].wait_recv()
                        ahead[way][chunk] = None
                    if step < steps or turn == 0:
                        ahead[way][chunk] = send(
                            block((me[axis] - way * (step - 1)) % SIZE[axis], chunk),
                            at(**{axis: me[axis] + way}),
                        )
            yield
        for way in (1, -1):
            for copy in ahead[way]:
                if copy is not None:
                    copy.wait_recv()

    def block_y(index, chunk):
        return dense_ref.at[0, pl.ds(8 * chunk, 8), index]

    def block_z(index, chunk):
        return dense_ref.at[1, 2 * index + chunk]

    whole_z = dense_ref.at[1, pl.ds(2 * z, 2)]
    pltpu.make_async_copy(whole_z, whole_z, one_sem.at[4]).wait()
    ring_z = ring("z", 4, block_z)
    next(ring_z)
    whole_y = dense_ref.at[0, :, y]
    pltpu.make_async_copy(whole_y, whole_y, one_sem.at[3]).wait()
    ring_y = ring("y", 2, block_y)
    next(ring_y)
    next(ring_z)
    next(ring_y)
    next(ring_z)
    next(ring_z)

    def region_fields(region):
        weights = (weight_ref[region, 0], weight_ref[region, 1])
        source = dense_ref.at[region].reshape(256 * 8, 128)
        target = field_ref.at[region].reshape(256 * 8, 128)
        index = group_x(me) if region == 0 else 8 + group_y(me)
        columns = pl.ds(pl.multiple_of(1024 * index, 1024), 1024)
        cols = jnp.concatenate([left_ref[:, columns], right_ref[:, columns]], axis=0)
        for t in range(0, 8, 2):
            pair = jnp.concatenate(
                [source[pl.ds(u, 256, stride=8), :] for u in (t, t + 1)], axis=1
            )
            field = dot3(weights, split(pair))
            field = field.reshape(16, 16, 256) * cols[None, :, t * 128 : t * 128 + 256]
            field = field.reshape(256, 256)
            for u in (0, 1):
                target[pl.ds(t + u, 256, stride=8), :] = field[:, u * 128 : u * 128 + 128]
        own = group_x(me) if region == 0 else group_y(me)
        landing = out_ref.at[:, pl.ds(pl.multiple_of(8 * index, 8), 8)]
        pltpu.make_async_copy(
            field_ref.at[region, pl.ds(32 * own, 32)], landing, one_sem.at[6]
        ).start()
        others = [(o, c) for o in range(4) for c in (0, 1) if (o, c) != (0, 0)]
        for o, c in others:
            if region == 0:
                target_at = at(x=x + o, core=(core + c) % 2)
                p = group_x(target_at)
            else:
                target_at = at(y=y + o, core=(core + c) % 2)
                p = group_y(target_at)
            pltpu.make_async_remote_copy(
                src_ref=field_ref.at[region, pl.ds(32 * p, 32)],
                dst_ref=landing,
                send_sem=one_sem.at[5],
                recv_sem=one_sem.at[6],
                device_id=device(target_at),
                device_id_type=MESH,
            ).start()

    for _ in ring_y:
        pass
    region_fields(0)
    for _ in ring_z:
        pass
    region_fields(1)
    pltpu.make_async_copy(out_ref, out_ref, one_sem.at[6]).wait()
    for copy in started:
        copy.wait_send()
    for region, count in ((0, 15), (1, 7)):
        sent = dense_ref.at[region, pl.ds(0, count), 0]
        pltpu.make_async_copy(sent, sent, one_sem.at[1 + region]).wait()
    sent = field_ref.at[:, pl.ds(0, 224)]
    pltpu.make_async_copy(sent, sent, one_sem.at[5]).wait()


def front(density, row_left, row_right, col_left, col_right):
    a, k = np.arange(256)[None, :], np.arange(256)[:, None]
    turn = np.stack(phase(a * (4 * k + 1), 1024, -1), axis=1).astype(np.float32)
    vmem = pl.BlockSpec(memory_space=pltpu.VMEM)
    return pl.pallas_call(
        front_kernel,
        out_shape=jax.ShapeDtypeStruct((32, 128, 128), F32),
        in_specs=[pl.BlockSpec(memory_space=pl.ANY)] + [vmem] * 5,
        out_specs=pl.BlockSpec(memory_space=pl.ANY),
        scratch_shapes=[
            pltpu.VMEM((4, 128, 128), F32),
            pltpu.VMEM((2, 16, 4, 4, 8, 128), F32),
            pltpu.VMEM((2, 2, 256, 256), BF16),
            pltpu.VMEM((2, 256, 8, 128), F32),
            pltpu.SemaphoreType.DMA((7,)),
            pltpu.SemaphoreType.DMA((24,)),
            pltpu.SemaphoreType.DMA((24,)),
        ],
        compiler_params=pltpu.CompilerParams(
            collective_id=0, has_side_effects=True, vmem_limit_bytes=40 << 20
        ),
    )(density, row_left, row_right, jnp.asarray(turn), col_left, col_right)


def columns_kernel(in_ref, lead_ref, twist_ref, trail_ref, back_trail_ref, back_lead_ref, out_ref, sum_ref):
    step = pl.program_id(0)

    def table(ref):
        return ref[0], ref[1]

    x = jnp.concatenate(
        [jnp.concatenate([in_ref[part, side, 0] for side in (0, 1)], axis=1) for part in (0, 1)], axis=0
    )
    y = dot3(table(lead_ref), split(x))
    spectra = []
    for side in (0, 1):
        real, imag = y[:256, side * 128 : side * 128 + 128], y[256:, side * 128 : side * 128 + 128]
        cos, sin = twist_ref[0], twist_ref[1]
        turned = jnp.concatenate([real * cos - imag * sin, real * sin + imag * cos], axis=1)
        spectra.append(dot3(split(turned), table(trail_ref)))
    left, right = spectra
    lr, li, rr, ri = left[:, :128], left[:, 128:], right[:, :128], right[:, 128:]
    product = jnp.concatenate([lr * rr - li * ri, lr * ri + li * rr], axis=1)

    @pl.when(step == 0)
    def _():
        sum_ref[...] = product

    @pl.when(step > 0)
    def _():
        sum_ref[...] += product

    @pl.when(step == pl.num_programs(0) - 1)
    def _():
        back = dot3(split(sum_ref[...]), table(back_trail_ref))
        real, imag = back[:, :128], back[:, 128:]
        cos, sin = twist_ref[0], twist_ref[1]
        turned = jnp.concatenate([real * cos + imag * sin, imag * cos - real * sin], axis=0)
        out_ref[...] = dot3(table(back_lead_ref), split(turned))


def columns(fields):
    lead, twist, trail, back_trail, back_lead = tables()

    def whole(array):
        return pl.BlockSpec(array.shape, lambda r: (0,) * array.ndim)

    constants = (lead, twist, trail, back_trail, back_lead)
    return pl.pallas_call(
        columns_kernel,
        out_shape=jax.ShapeDtypeStruct((256, 128), F32),
        grid=(8,),
        in_specs=[pl.BlockSpec((2, 2, 1, 128, 128), lambda r: (0, 0, r, 0, 0))]
        + [whole(c) for c in constants],
        out_specs=pl.BlockSpec((256, 128), lambda r: (0, 0)),
        scratch_shapes=[pltpu.VMEM((256, 256), F32)],
        compiler_params=pltpu.CompilerParams(vmem_limit_bytes=40 << 20),
    )(fields.reshape(2, 2, 8, 128, 128), *(jnp.asarray(c) for c in constants))


def finish_kernel(q_ref, rows_ref, mix_ref, out_ref, got_ref, part_ref, all_ref, line_ref, sems):
    comp, rank = lax.axis_index("comp"), lax.axis_index("rank")

    def peer(offset):
        return {"comp": (comp + offset) % 64, "rank": rank}

    def other(offset):
        return {"comp": comp, "rank": (rank + offset) % 4}

    barrier = pltpu.get_barrier_semaphore()

    def greet(i, carry):
        pl.semaphore_signal(barrier, inc=1, device_id=peer(i), device_id_type=MESH)
        return carry

    lax.fori_loop(1, 64, greet, 0)
    for i in range(1, 4):
        pl.semaphore_signal(barrier, inc=1, device_id=other(i), device_id_type=MESH)
    pl.semaphore_wait(barrier, 66)

    def exchange(source, target, send_sem, recv_sem):
        own = pltpu.make_async_copy(source.at[comp], target.at[comp], recv_sem)
        own.start()

        def send(i, carry):
            to = peer(i)
            pltpu.make_async_remote_copy(
                src_ref=source.at[to["comp"]],
                dst_ref=target.at[comp],
                send_sem=send_sem,
                recv_sem=recv_sem,
                device_id=to,
                device_id_type=MESH,
            ).start()
            return carry

        lax.fori_loop(1, 64, send, 0)
        pltpu.make_async_copy(source, target, recv_sem).wait()
        rest = pl.ds(0, 63)
        pltpu.make_async_copy(source.at[rest], target.at[rest], send_sem).wait()

    exchange(q_ref, got_ref, sems.at[0], sems.at[1])
    x = jnp.concatenate(
        [
            jnp.concatenate([got_ref[:, 2 * part + t, :] for t in (0, 1)], axis=1)
            for part in (0, 1)
        ],
        axis=0,
    )
    part = dot3((rows_ref[0], rows_ref[1]), split(x))
    for q in range(4):
        part_ref[q] = part[32 * q : 32 * q + 32]
    own = pltpu.make_async_copy(part_ref.at[rank], all_ref.at[rank], sems.at[2])
    own.start()
    copies = []
    for i in range(1, 4):
        to = other(i)
        copy = pltpu.make_async_remote_copy(
            src_ref=part_ref.at[to["rank"]],
            dst_ref=all_ref.at[rank],
            send_sem=sems.at[3 + i],
            recv_sem=sems.at[6 + i],
            device_id=to,
            device_id_type=MESH,
        )
        copy.start()
        copies.append(copy)
    own.wait()
    for copy in copies:
        copy.wait()
    lines = dot3((mix_ref[0, rank], mix_ref[1, rank]), split(all_ref[...].reshape(128, 256)))
    for t in (0, 1):
        line_ref[:, t, :] = lines[:, t * 128 : t * 128 + 128]
    exchange(line_ref, out_ref, sems.at[3], sems.at[10])


def finish(q, total):
    rows_table, mix = final_tables(total)
    vmem = pl.BlockSpec(memory_space=pltpu.VMEM)
    return pl.pallas_call(
        finish_kernel,
        out_shape=jax.ShapeDtypeStruct((64, 2, 128), F32),
        in_specs=[vmem] * 3,
        out_specs=vmem,
        scratch_shapes=[
            pltpu.VMEM((64, 4, 128), F32),
            pltpu.VMEM((4, 32, 256), F32),
            pltpu.VMEM((4, 32, 256), F32),
            pltpu.VMEM((64, 2, 128), F32),
            pltpu.SemaphoreType.DMA((11,)),
        ],
        compiler_params=pltpu.CompilerParams(
            collective_id=1, has_side_effects=True, vmem_limit_bytes=40 << 20
        ),
    )(q.reshape(64, 4, 128), jnp.asarray(rows_table), jnp.asarray(mix))


def body(density, row_left, col_left, row_right, col_right):
    lines = density.reshape(4, 128, 128).transpose(1, 0, 2)
    fields = front(lines, row_left, row_right, col_left, col_right)
    return finish(columns(fields), 256 * 16384).reshape(1, 16384)


def solution(mesh):
    return jax.shard_map(
        body,
        mesh=mesh,
        in_specs=(P("comp", None), P(), P(), P(), P()),
        out_specs=P(("comp", "rank"), None),
        check_vma=False,
    )
```

```python
import functools
import math

import jax
import jax.numpy as jnp
import ml_dtypes
import numpy as np
from jax import lax
from jax.experimental import pallas as pl
from jax.experimental.pallas import tpu as pltpu
from jax.sharding import PartitionSpec as P

MESH = pl.DeviceIdType.MESH
BF16 = jnp.bfloat16
F32 = jnp.float32
SIZE = {"x": 4, "y": 4, "z": 8}


def halves(table):
    table = np.asarray(table, np.float64)
    high = table.astype(ml_dtypes.bfloat16)
    low = (table - high.astype(np.float64)).astype(ml_dtypes.bfloat16)
    return np.stack([high, low])


def phase(numerator, length, sign):
    angle = sign * 2.0 * np.pi * (np.asarray(numerator) % length) / length
    return np.cos(angle), np.sin(angle)


def as_real(cos, sin):
    return np.block([[cos, -sin], [sin, cos]])


def tables(total):
    k1, t1 = np.arange(256)[:, None], np.arange(128)[None, :]
    k2, s = np.arange(128)[:, None], np.arange(128)[None, :]
    a, k = np.arange(256)[None, :], np.arange(256)[:, None]
    turn = np.stack(phase(a * (4 * k + 1), 1024, -1), axis=1).astype(np.float32)
    lead = as_real(*phase(k1 * t1, 256, -1))
    twist = np.stack(phase(k1 * s, 32768, -1)).astype(np.float32)
    trail = as_real(*phase(k2 * s, 128, -1)).T
    back_trail = as_real(*phase(k2 * s, 128, 1)).T
    back_lead = as_real(*phase(np.arange(128)[:, None] * np.arange(256)[None, :], 256, 1))
    order = [8 * i + t + 128 * part for i in range(16) for part in (0, 1) for t in range(8)]
    back_lead = back_lead[np.array(order)]
    scale = 0.5 / (math.sqrt(total) * 256.0 * 32768.0)
    j, a0 = np.arange(16)[:, None], np.arange(16)[None, :]
    middle = scale * np.stack(phase(a0 * (4 * j + 1), 1024, 1), axis=2).reshape(16, 32, 1)
    middle = np.broadcast_to(middle, (16, 32, 128)).astype(np.float32)
    return turn, halves(lead), twist, halves(trail), halves(back_trail), halves(back_lead), middle


def scaled(value, numerator, length):
    real, imag = value
    cos, sin = (float(v) for v in phase(numerator, length, 1))
    if numerator == 0:
        return value
    if 4 * numerator == length:
        return -imag, real
    return real * cos - imag * sin, real * sin + imag * cos


def short_dft(values):
    length = len(values)
    if length == 1:
        return values
    even, odd = short_dft(values[0::2]), short_dft(values[1::2])
    odd = [scaled(v, n, length) for n, v in enumerate(odd)]
    pairs = list(zip(even, odd))
    return [(e[0] + o[0], e[1] + o[1]) for e, o in pairs] + [
        (e[0] - o[0], e[1] - o[1]) for e, o in pairs
    ]


def split(value):
    high = value.astype(BF16)
    return high, (value - high.astype(F32)).astype(BF16)


def dot3(first, second):
    dot = functools.partial(jnp.dot, preferred_element_type=F32)
    return dot(first[0], second[0]) + (dot(first[0], second[1]) + dot(first[1], second[0]))


def place():
    comp, rank = lax.axis_index("comp"), lax.axis_index("rank")
    return {"z": comp // 8, "y": comp % 4, "x": rank // 2 * 2 + comp // 4 % 2, "core": rank % 2}


def device(at):
    return {"comp": (at["z"] * 2 + at["x"] % 2) * 4 + at["y"], "rank": at["x"] // 2 * 2 + at["core"]}


def kernel(
    d_ref, row_left_ref, row_right_ref, left_ref, right_ref,
    turn_hbm, lead_hbm, twist_hbm, trail_hbm, back_trail_hbm, back_lead_hbm, middle_hbm,
    out_ref,
    lines_ref, dense_ref, weight_ref, field_ref, all_ref, cols_ref,
    turn_ref, lead_ref, twist_ref, trail_ref, back_trail_ref, back_lead_ref, middle_ref,
    sum_ref, conv_ref, got_ref, part_ref, line_ref,
    one_sem, send_sem, recv_sem,
):
    me = place()
    z, y, x, core = me["z"], me["y"], me["x"], me["core"]
    mine = (z * 2 + x % 2, y)

    def at(**changes):
        moved = dict(me)
        for axis, value in changes.items():
            moved[axis] = value % SIZE[axis] if axis in SIZE else value
        return moved

    def group_x(where):
        return where["x"] % 2 * 4 + where["x"] // 2 * 2 + where["core"]

    def group_y(where):
        return where["y"] * 2 + where["core"]

    def group(region, where):
        return group_x(where) if region == 0 else group_y(where)

    def member(region, p):
        if region == 0:
            return at(x=p // 4 + p % 4 // 2 * 2, core=p % 2)
        return at(y=p // 2, core=p % 2)

    for row in range(4):
        pltpu.make_async_copy(d_ref.at[:, row], lines_ref.at[row], one_sem.at[0]).start()
    barrier = pltpu.get_barrier_semaphore()
    friends = [at(z=z + o) for o in range(1, 8)]
    friends += [at(z=z + o, x=x + side) for o in range(8) for side in (1, -1)]
    friends += [at(y=y + o) for o in range(1, 4)]
    friends += [at(y=y + o, x=x + side) for o in range(1, 4) for side in (1, -1)]
    friends += [at(x=x + 2)]
    friends += [at(x=x + o, core=1 - core) for o in range(4)]
    friends += [at(y=y + o, core=1 - core) for o in range(1, 4)]
    friends += [at(y=y + o, x=x + 2, core=c) for o in range(1, 4) for c in (0, 1)]
    for friend in friends:
        pl.semaphore_signal(barrier, inc=1, device_id=device(friend), device_id_type=MESH)

    for region in (0, 1):
        for p in range(8):
            owner = device(member(region, p))
            pltpu.make_async_copy(
                turn_hbm.at[4 * owner["comp"] + owner["rank"]],
                turn_ref.at[8 * region + p],
                one_sem.at[7],
            ).start()
    for region in (0, 1):
        columns = pl.ds(pl.multiple_of(1024 * (8 * region + group(region, me)), 1024), 1024)
        for side, source in enumerate((left_ref, right_ref)):
            pltpu.make_async_copy(
                source.at[:, columns], cols_ref.at[region, pl.ds(8 * side, 8)], one_sem.at[8]
            ).start()
    mine_j = y * 4 + x // 2 * 2 + core
    mine_i = z * 2 + x % 2
    for source, target in (
        (lead_hbm, lead_ref),
        (twist_hbm, twist_ref),
        (trail_hbm, trail_ref),
        (back_trail_hbm, back_trail_ref),
        (back_lead_hbm, back_lead_ref),
        (middle_hbm.at[mine_j], middle_ref),
    ):
        pltpu.make_async_copy(source, target, one_sem.at[9]).start()
    pltpu.make_async_copy(turn_ref, turn_ref, one_sem.at[7]).wait()
    both = jnp.concatenate([row_left_ref[...], row_right_ref[...]], axis=0)
    for region in (0, 1):
        for p in range(8):
            turn = turn_ref[8 * region + p]
            for part in (0, 1):
                high, low = split(both * turn[part : part + 1])
                first = 32 * p + 16 * part
                weight_ref[region, 0, first : first + 16] = high
                weight_ref[region, 1, first : first + 16] = low

    pltpu.make_async_copy(lines_ref, lines_ref, one_sem.at[0]).wait()
    pl.semaphore_wait(barrier, len(friends))

    def slices(region, where):
        index = group_x(where) if region == 0 else 8 + group_y(where)
        return lines_ref.at[:, pl.ds(pl.multiple_of(8 * index, 8), 8)]

    def spread(region, targets):
        pltpu.make_async_copy(
            slices(region, me), dense_ref.at[(region,) + mine], one_sem.at[3 + region]
        ).start()
        for target in targets:
            pltpu.make_async_remote_copy(
                src_ref=slices(region, target),
                dst_ref=dense_ref.at[(region,) + mine],
                send_sem=one_sem.at[1 + region],
                recv_sem=one_sem.at[3 + region],
                device_id=device(target),
                device_id_type=MESH,
            ).start()

    spread(
        1,
        [at(y=y + o) for o in range(1, 4)]
        + [at(y=y + o, x=x - 1 + (y + o) % 4 % 2 * 2) for o in range(4)],
    )
    spread(
        0,
        [at(z=z + o) for o in range(1, 8)]
        + [at(z=z + o, x=x - 1 + (z + o) % 8 % 2 * 2) for o in range(8)],
    )
    started = []

    def send(block, target):
        i = len(started)
        copy = pltpu.make_async_remote_copy(
            src_ref=block,
            dst_ref=block,
            send_sem=send_sem.at[i],
            recv_sem=recv_sem.at[i],
            device_id=device(target),
            device_id_type=MESH,
        )
        copy.start()
        started.append(copy)
        return copy

    def ring(axis, steps, block):
        ahead = {1: [None, None], -1: [None, None]}
        for step in range(1, steps + 1):
            for turn in (0, 1):
                for way in (1, -1):
                    chunk = turn if way == 1 else 1 - turn
                    if ahead[way][chunk] is not None:
                        ahead[way][chunk].wait_recv()
                        ahead[way][chunk] = None
                    if step < steps or turn == 0:
                        ahead[way][chunk] = send(
                            block((me[axis] - way * (step - 1)) % SIZE[axis], chunk),
                            at(**{axis: me[axis] + way}),
                        )
            yield
        for way in (1, -1):
            for copy in ahead[way]:
                if copy is not None:
                    copy.wait_recv()

    def block_y(index, chunk):
        return dense_ref.at[0, pl.ds(8 * chunk, 8), index]

    def block_z(index, chunk):
        return dense_ref.at[1, 2 * index + chunk]

    whole_z = dense_ref.at[1, pl.ds(2 * z, 2)]
    pltpu.make_async_copy(whole_z, whole_z, one_sem.at[4]).wait()
    ring_z = ring("z", 4, block_z)
    next(ring_z)
    whole_y = dense_ref.at[0, :, y]
    pltpu.make_async_copy(whole_y, whole_y, one_sem.at[3]).wait()
    ring_y = ring("y", 2, block_y)
    next(ring_y)
    next(ring_z)
    next(ring_y)
    next(ring_z)
    next(ring_z)

    counts = (1, 4)

    def region_fields(region):
        weights = (weight_ref[region, 0], weight_ref[region, 1])
        source = dense_ref.at[region].reshape(256 * 8, 128)
        target = field_ref.at[region].reshape(256 * 8, 128)
        for t in range(0, 8, 2):
            pair = jnp.concatenate(
                [source[pl.ds(u, 256, stride=8), :] for u in (t, t + 1)], axis=1
            )
            field = dot3(weights, split(pair))
            cols = cols_ref[region, :, t * 128 : t * 128 + 256]
            field = (field.reshape(16, 16, 256) * cols[None]).reshape(256, 256)
            for u in (0, 1):
                target[pl.ds(t + u, 256, stride=8), :] = field[:, u * 128 : u * 128 + 128]
        own = group(region, me)
        place_t = pl.ds(pl.multiple_of(64 * region + 8 * own, 8), 8)
        terms = 8 // counts[region]
        for chunk in range(counts[region]):
            which = pl.ds(terms * chunk, terms)
            landing = all_ref.at[:, which, place_t]
            recv = one_sem.at[10 + 4 * region + chunk]
            pltpu.make_async_copy(field_ref.at[region, own, :, which], landing, recv).start()
            for o, c in [(2, 0), (2, 1), (1, 0), (3, 1), (1, 1), (3, 0), (0, 1)]:
                moved = {"core": (core + c) % 2, "xy"[region]: me["xy"[region]] + o}
                moved = at(**moved)
                pltpu.make_async_remote_copy(
                    src_ref=field_ref.at[region, group(region, moved), :, which],
                    dst_ref=landing,
                    send_sem=one_sem.at[5],
                    recv_sem=recv,
                    device_id=device(moved),
                    device_id_type=MESH,
                ).start()

    def arrived(region, chunk):
        terms = 8 // counts[region]
        block = all_ref.at[:, pl.ds(terms * chunk, terms), pl.ds(64 * region, 64)]
        pltpu.make_async_copy(block, block, one_sem.at[10 + 4 * region + chunk]).wait()

    def table(ref):
        return ref[0], ref[1]

    def convolve(r, carry):
        x = jnp.concatenate(
            [
                jnp.concatenate([all_ref[2 * part + side, r] for side in (0, 1)], axis=1)
                for part in (0, 1)
            ],
            axis=0,
        )
        y = dot3(table(lead_ref), split(x))
        spectra = []
        for side in (0, 1):
            lanes = slice(side * 128, side * 128 + 128)
            real, imag = y[:256, lanes], y[256:, lanes]
            cos, sin = twist_ref[0], twist_ref[1]
            turned = jnp.concatenate([real * cos - imag * sin, real * sin + imag * cos], axis=1)
            spectra.append(dot3(split(turned), table(trail_ref)))
        left, right = spectra
        lr, li, rr, ri = left[:, :128], left[:, 128:], right[:, :128], right[:, 128:]
        sum_ref[:, :128] += lr * rr - li * ri
        sum_ref[:, 128:] += lr * ri + li * rr
        return carry

    pltpu.make_async_copy(cols_ref, cols_ref, one_sem.at[8]).wait()
    for _ in ring_y:
        pass
    region_fields(0)
    for _ in ring_z:
        pass
    region_fields(1)
    sum_ref[...] = jnp.zeros_like(sum_ref)
    for target in (lead_ref, twist_ref, trail_ref, back_trail_ref, back_lead_ref, middle_ref):
        pltpu.make_async_copy(target, target, one_sem.at[9]).wait()
    arrived(0, 0)
    for chunk in range(4):
        arrived(1, chunk)
        lax.fori_loop(2 * chunk, 2 * chunk + 2, convolve, 0)

    back = dot3(split(sum_ref[...]), table(back_trail_ref))
    real, imag = back[:, :128], back[:, 128:]
    cos, sin = twist_ref[0], twist_ref[1]
    turned = jnp.concatenate([real * cos + imag * sin, imag * cos - real * sin], axis=0)
    conv_ref[...] = dot3(table(back_lead_ref), split(turned)).reshape(16, 16, 128)

    def by_i(i):
        return at(z=i // 2, x=x // 2 * 2 + i % 2)

    def by_j(j):
        return at(y=j // 4, x=j % 4 // 2 * 2 + x % 2, core=j % 2)

    def exchange(source, target, to, own, sems):
        pltpu.make_async_copy(source.at[own], target.at[own], sems[1]).start()
        for o in range(1, 16):
            index = (own + o) % 16
            pltpu.make_async_remote_copy(
                src_ref=source.at[index],
                dst_ref=target.at[own],
                send_sem=sems[0],
                recv_sem=sems[1],
                device_id=device(to(index)),
                device_id_type=MESH,
            ).start()
        pltpu.make_async_copy(target, target, sems[1]).wait()

    exchange(conv_ref, got_ref.at[0], by_i, mine_i, (one_sem.at[18], one_sem.at[19]))
    values = [(got_ref[0, i, :8], got_ref[0, i, 8:]) for i in range(16)]
    for a, (real, imag) in enumerate(short_dft(values)):
        cos, sin = middle_ref[2 * a : 2 * a + 1], middle_ref[2 * a + 1 : 2 * a + 2]
        part_ref[a, :8] = real * cos - imag * sin
        part_ref[a, 8:] = real * sin + imag * cos
    exchange(part_ref, got_ref.at[1], by_j, mine_j, (one_sem.at[20], one_sem.at[21]))
    values = [(got_ref[1, i, :8], got_ref[1, i, 8:]) for i in range(16)]
    for a, value in enumerate(short_dft(values)):
        line_ref[a] = scaled(value, a, 64)[0]
    exchange(line_ref, out_ref, by_i, mine_i, (one_sem.at[22], one_sem.at[23]))

    for copy in started:
        copy.wait_send()
    for region, count in ((0, 15), (1, 7)):
        sent = dense_ref.at[region, pl.ds(0, count), 0]
        pltpu.make_async_copy(sent, sent, one_sem.at[1 + region]).wait()
    sent = field_ref.at[:, pl.ds(0, 7)]
    pltpu.make_async_copy(sent, sent, one_sem.at[5]).wait()
    for source, sem in ((conv_ref, 18), (part_ref, 20), (line_ref, 22)):
        sent = source.at[pl.ds(0, 15)]
        pltpu.make_async_copy(sent, sent, one_sem.at[sem]).wait()


def body(density, row_left, col_left, row_right, col_right):
    lines = density.reshape(4, 128, 128).transpose(1, 0, 2)
    constants = [jnp.asarray(c) for c in tables(256 * 16384)]
    vmem = pl.BlockSpec(memory_space=pltpu.VMEM)
    here = pl.BlockSpec(memory_space=pl.ANY)
    out = pl.pallas_call(
        kernel,
        out_shape=jax.ShapeDtypeStruct((16, 8, 128), F32),
        in_specs=[here, vmem, vmem] + [here] * 9,
        out_specs=here,
        scratch_shapes=[
            pltpu.VMEM((4, 128, 128), F32),
            pltpu.VMEM((2, 16, 4, 4, 8, 128), F32),
            pltpu.VMEM((2, 2, 256, 256), BF16),
            pltpu.VMEM((2, 8, 4, 8, 8, 128), F32),
            pltpu.VMEM((4, 8, 128, 128), F32),
            pltpu.VMEM((2, 16, 1024), F32),
            pltpu.VMEM((16, 2, 256), F32),
            pltpu.VMEM((2, 512, 256), BF16),
            pltpu.VMEM((2, 256, 128), F32),
            pltpu.VMEM((2, 256, 256), BF16),
            pltpu.VMEM((2, 256, 256), BF16),
            pltpu.VMEM((2, 256, 512), BF16),
            pltpu.VMEM((32, 128), F32),
            pltpu.VMEM((256, 256), F32),
            pltpu.VMEM((16, 16, 128), F32),
            pltpu.VMEM((2, 16, 16, 128), F32),
            pltpu.VMEM((16, 16, 128), F32),
            pltpu.VMEM((16, 8, 128), F32),
            pltpu.SemaphoreType.DMA((24,)),
            pltpu.SemaphoreType.DMA((24,)),
            pltpu.SemaphoreType.DMA((24,)),
        ],
        compiler_params=pltpu.CompilerParams(
            collective_id=0, has_side_effects=True, vmem_limit_bytes=60 << 20
        ),
    )(lines, row_left, row_right, col_left, col_right, *constants)
    return out.reshape(1, 16384)


def solution(mesh):
    return jax.shard_map(
        body,
        mesh=mesh,
        in_specs=(P("comp", None), P(), P(), P(), P()),
        out_specs=P(("comp", "rank"), None),
        check_vma=False,
    )
```

```python
import functools
import math

import jax
import jax.numpy as jnp
import ml_dtypes
import numpy as np
from jax import lax
from jax.experimental import pallas as pl
from jax.experimental.pallas import tpu as pltpu
from jax.sharding import PartitionSpec as P

MESH = pl.DeviceIdType.MESH
BF16 = jnp.bfloat16
F32 = jnp.float32
SIZE = {"x": 4, "y": 4, "z": 8}
AHEAD = 4


def halves(table):
    table = np.asarray(table, np.float64)
    high = table.astype(ml_dtypes.bfloat16)
    low = (table - high.astype(np.float64)).astype(ml_dtypes.bfloat16)
    return np.stack([high, low])


def phase(numerator, length, sign):
    angle = sign * 2.0 * np.pi * (np.asarray(numerator) % length) / length
    return np.cos(angle), np.sin(angle)


def as_real(cos, sin):
    return np.block([[cos, -sin], [sin, cos]])


def tables(total):
    k1, t1 = np.arange(256)[:, None], np.arange(128)[None, :]
    k2, s = np.arange(128)[:, None], np.arange(128)[None, :]
    a, k = np.arange(256)[None, :], np.arange(256)[:, None]
    turn = np.stack(phase(a * (4 * k + 1), 1024, -1), axis=1).astype(np.float32)
    lead = as_real(*phase(k1 * t1, 256, -1))
    twist = np.stack(phase(k1 * s, 32768, -1)).astype(np.float32)
    trail = as_real(*phase(k2 * s, 128, -1)).T
    back_trail = as_real(*phase(k2 * s, 128, 1)).T
    back_lead = as_real(*phase(np.arange(128)[:, None] * np.arange(256)[None, :], 256, 1))
    order = [8 * i + t + 128 * part for i in range(16) for part in (0, 1) for t in range(8)]
    back_lead = back_lead[np.array(order)]
    scale = 0.5 / (math.sqrt(total) * 256.0 * 32768.0)
    j, a0 = np.arange(16)[:, None], np.arange(16)[None, :]
    middle = scale * np.stack(phase(a0 * (4 * j + 1), 1024, 1), axis=2).reshape(16, 32, 1)
    middle = np.broadcast_to(middle, (16, 32, 128)).astype(np.float32)
    return turn, halves(lead), twist, halves(trail), halves(back_trail), halves(back_lead), middle


def scaled(value, numerator, length):
    real, imag = value
    cos, sin = (float(v) for v in phase(numerator, length, 1))
    if numerator == 0:
        return value
    if 4 * numerator == length:
        return -imag, real
    return real * cos - imag * sin, real * sin + imag * cos


def short_dft(values):
    length = len(values)
    if length == 1:
        return values
    even, odd = short_dft(values[0::2]), short_dft(values[1::2])
    odd = [scaled(v, n, length) for n, v in enumerate(odd)]
    pairs = list(zip(even, odd))
    return [(e[0] + o[0], e[1] + o[1]) for e, o in pairs] + [
        (e[0] - o[0], e[1] - o[1]) for e, o in pairs
    ]


def split(value):
    high = value.astype(BF16)
    return high, (value - high.astype(F32)).astype(BF16)


def dot3(first, second):
    dot = functools.partial(jnp.dot, preferred_element_type=F32)
    return dot(first[0], second[0]) + (dot(first[0], second[1]) + dot(first[1], second[0]))


def place():
    comp, rank = lax.axis_index("comp"), lax.axis_index("rank")
    return {"z": comp // 8, "y": comp % 4, "x": rank // 2 * 2 + comp // 4 % 2, "core": rank % 2}


def device(at):
    return {"comp": (at["z"] * 2 + at["x"] % 2) * 4 + at["y"], "rank": at["x"] // 2 * 2 + at["core"]}


def kernel(
    d_ref, row_left_ref, row_right_ref, left_ref, right_ref,
    turn_hbm, lead_hbm, twist_hbm, trail_hbm, back_trail_hbm, back_lead_hbm, middle_hbm,
    out_ref,
    lines_ref, dense_ref, weight_ref, field_ref, all_ref, cols_ref,
    turn_ref, lead_ref, twist_ref, trail_ref, back_trail_ref, back_lead_ref, middle_ref,
    sum_ref, conv_ref, got_ref, part_ref, line_ref,
    one_sem, send_sem, recv_sem, pair_sem,
):
    me = place()
    z, y, x, core = me["z"], me["y"], me["x"], me["core"]
    mine = (z * 2 + x % 2, y)

    def at(**changes):
        moved = dict(me)
        for axis, value in changes.items():
            moved[axis] = value % SIZE[axis] if axis in SIZE else value
        return moved

    def group_x(where):
        return where["x"] % 2 * 4 + where["x"] // 2 * 2 + where["core"]

    def group_y(where):
        return where["y"] * 2 + where["core"]

    def group(region, where):
        return group_x(where) if region == 0 else group_y(where)

    def member(region, p):
        if region == 0:
            return at(x=p // 4 + p % 4 // 2 * 2, core=p % 2)
        return at(y=p // 2, core=p % 2)

    for row in range(4):
        pltpu.make_async_copy(d_ref.at[:, :, row], lines_ref.at[:, row], one_sem.at[0]).start()
    barrier = pltpu.get_barrier_semaphore()
    friends = [at(z=z + o) for o in range(1, 8)]
    friends += [at(y=y + o) for o in range(1, 4)]
    friends += [at(x=x + o) for o in range(1, 4)]
    friends += [at(core=1 - core)]
    for friend in friends:
        pl.semaphore_signal(barrier, inc=1, device_id=device(friend), device_id_type=MESH)

    for region in (0, 1):
        for p in range(8):
            owner = device(member(region, p))
            pltpu.make_async_copy(
                turn_hbm.at[4 * owner["comp"] + owner["rank"]],
                turn_ref.at[8 * region + p],
                one_sem.at[7],
            ).start()
    for region in (0, 1):
        columns = pl.ds(pl.multiple_of(1024 * (8 * region + group(region, me)), 1024), 1024)
        for side, source in enumerate((left_ref, right_ref)):
            pltpu.make_async_copy(
                source.at[:, columns], cols_ref.at[region, pl.ds(8 * side, 8)], one_sem.at[8]
            ).start()
    mine_j = y * 4 + x // 2 * 2 + core
    mine_i = z * 2 + x % 2
    for source, target in (
        (lead_hbm, lead_ref),
        (twist_hbm, twist_ref),
        (trail_hbm, trail_ref),
        (back_trail_hbm, back_trail_ref),
        (back_lead_hbm, back_lead_ref),
        (middle_hbm.at[mine_j], middle_ref),
    ):
        pltpu.make_async_copy(source, target, one_sem.at[9]).start()
    pltpu.make_async_copy(turn_ref, turn_ref, one_sem.at[7]).wait()
    both = jnp.concatenate([row_left_ref[...], row_right_ref[...]], axis=0)
    for region in (0, 1):
        for p in range(8):
            turn = turn_ref[8 * region + p]
            for part in (0, 1):
                high, low = split(both * turn[part : part + 1])
                first = 32 * p + 16 * part
                weight_ref[region, 0, first : first + 16] = high
                weight_ref[region, 1, first : first + 16] = low

    pltpu.make_async_copy(lines_ref, lines_ref, one_sem.at[0]).wait()
    pl.semaphore_wait(barrier, len(friends))
    pl.semaphore_signal(
        pair_sem, inc=1, device_id=device(at(core=1 - core)), device_id_type=MESH
    )

    def slices(region, where):
        return lines_ref.at[8 * region + group(region, where)]

    def copy(source, block, sender, receiver, target):
        pltpu.make_async_remote_copy(
            src_ref=source,
            dst_ref=block,
            send_sem=sender,
            recv_sem=receiver,
            device_id=device(target),
            device_id_type=MESH,
        ).start()

    def await_block(block, sem):
        pltpu.make_async_copy(block, block, sem).wait()

    near = [1, 7, 2, 6, 3, 5, 4]
    first_block = dense_ref.at[(0,) + mine]
    second_block = dense_ref.at[(1,) + mine]
    beside = at(x=x - 1 + z % 2 * 2)
    copy(slices(0, beside), first_block, one_sem.at[1], one_sem.at[24], beside)
    for o in range(1, 4):
        target = at(y=y + o)
        copy(slices(1, target), second_block, one_sem.at[2], one_sem.at[4], target)
    for o in near:
        copy(slices(0, me), first_block, one_sem.at[1], one_sem.at[24 + o], at(z=z + o))
    own = pltpu.make_async_copy(slices(0, me), first_block, one_sem.at[3])
    own.start()
    pltpu.make_async_copy(slices(1, me), second_block, one_sem.at[4]).start()
    started = []

    def send(block, target):
        i = len(started)
        copy = pltpu.make_async_remote_copy(
            src_ref=block,
            dst_ref=block,
            send_sem=send_sem.at[i],
            recv_sem=recv_sem.at[i],
            device_id=device(target),
            device_id_type=MESH,
        )
        copy.start()
        started.append(copy)
        return copy

    def ring(axis, steps, block):
        ahead = {1: [None, None], -1: [None, None]}
        for step in range(1, steps + 1):
            for turn in (0, 1):
                for way in (1, -1):
                    chunk = turn if way == 1 else 1 - turn
                    if ahead[way][chunk] is not None:
                        ahead[way][chunk].wait_recv()
                        ahead[way][chunk] = None
                    if step < steps or turn == 0:
                        ahead[way][chunk] = send(
                            block((me[axis] - way * (step - 1)) % SIZE[axis], chunk),
                            at(**{axis: me[axis] + way}),
                        )
            yield
        for way in (1, -1):
            for copy in ahead[way]:
                if copy is not None:
                    copy.wait_recv()

    def block_z(index, chunk):
        return dense_ref.at[1, 2 * index + x % 2, pl.ds(2 * chunk, 2)]

    def along_y(o):
        block = dense_ref.at[0, pl.ds((z - o) % 8 * 2, 2), y]
        if o:
            await_block(block, one_sem.at[24 + o])
        for step in (2, 1, 3):
            copy(block, block, one_sem.at[32], one_sem.at[33], at(y=y + step))

    def along_x(o):
        index = (z + o) % 8
        block = dense_ref.at[1, 2 * index + x % 2]
        copy(block, block, one_sem.at[34], one_sem.at[35], at(x=x + 1 - index % 2 * 2))

    other_block = dense_ref.at[0, z * 2 + 1 - x % 2, y]
    await_block(other_block, one_sem.at[24])
    for o in near:
        copy(other_block, other_block, one_sem.at[36], one_sem.at[24 + o], at(z=z + o))
    own.wait()
    along_y(0)
    await_block(dense_ref.at[1, z * 2 + x % 2], one_sem.at[4])
    ring_z = ring("z", 4, block_z)
    next(ring_z)
    along_x(0)
    for step in (1, 2, 3):
        next(ring_z)
        along_x(step)
        along_x(-step)
        along_y(step)
        along_y(8 - step)
    along_y(4)
    for _ in ring_z:
        pass
    along_x(4)

    counts = (1, 4)

    def region_fields(region):
        weights = (weight_ref[region, 0], weight_ref[region, 1])
        source = dense_ref.at[region].reshape(256 * 8, 128)
        target = field_ref.at[region].reshape(256 * 8, 128)
        for t in range(0, 8, 2):
            pair = jnp.concatenate(
                [source[pl.ds(u, 256, stride=8), :] for u in (t, t + 1)], axis=1
            )
            field = dot3(weights, split(pair))
            cols = cols_ref[region, :, t * 128 : t * 128 + 256]
            field = (field.reshape(16, 16, 256) * cols[None]).reshape(256, 256)
            for u in (0, 1):
                lanes = slice(u * 128, u * 128 + 128)
                for p in range(8):
                    for kind in range(4):
                        low = 32 * p + 8 * kind
                        at_rows = pl.ds(256 * p + 8 * kind + t + u, 8, stride=32)
                        target[at_rows, :] = field[low : low + 8, lanes]

    def send_fields(region, chunk):
        own = group(region, me)
        terms = 8 // counts[region]
        which = pl.ds(terms * chunk, terms)
        landing = all_ref.at[8 * region + own, which]
        recv = one_sem.at[10 + 4 * region + chunk]
        pltpu.make_async_copy(field_ref.at[region, own, which], landing, recv).start()
        for o, c in [(2, 0), (2, 1), (1, 0), (3, 1), (1, 1), (3, 0), (0, 1)]:
            moved = {"core": (core + c) % 2, "xy"[region]: me["xy"[region]] + o}
            moved = at(**moved)
            source = field_ref.at[region, group(region, moved), which]
            copy(source, landing, one_sem.at[5], recv, moved)

    def arrived(region, chunk):
        terms = 8 // counts[region]
        block = all_ref.at[pl.ds(8 * region, 8), pl.ds(terms * chunk, terms)]
        pltpu.make_async_copy(block, block, one_sem.at[10 + 4 * region + chunk]).wait()

    def table(ref):
        return ref[0], ref[1]

    def convolve(r):
        x = jnp.concatenate(
            [
                jnp.concatenate([all_ref[:, r, 2 * part + side].reshape(128, 128) for side in (0, 1)], axis=1)
                for part in (0, 1)
            ],
            axis=0,
        )
        y = dot3(table(lead_ref), split(x))
        spectra = []
        for side in (0, 1):
            lanes = slice(side * 128, side * 128 + 128)
            real, imag = y[:256, lanes], y[256:, lanes]
            cos, sin = twist_ref[0], twist_ref[1]
            turned = jnp.concatenate([real * cos - imag * sin, real * sin + imag * cos], axis=1)
            spectra.append(dot3(split(turned), table(trail_ref)))
        left, right = spectra
        lr, li, rr, ri = left[:, :128], left[:, 128:], right[:, :128], right[:, 128:]
        sum_ref[:, :128] += lr * rr - li * ri
        sum_ref[:, 128:] += lr * ri + li * rr

    pltpu.make_async_copy(cols_ref, cols_ref, one_sem.at[8]).wait()
    await_block(dense_ref.at[0, :, pl.ds(0, 3)], one_sem.at[33])
    pl.semaphore_wait(pair_sem, 1)
    region_fields(0)
    send_fields(0, 0)
    await_block(dense_ref.at[1, pl.ds(0, 8)], one_sem.at[35])
    region_fields(1)
    for chunk in range(AHEAD):
        send_fields(1, chunk)
    sum_ref[...] = jnp.zeros_like(sum_ref)
    for target in (lead_ref, twist_ref, trail_ref, back_trail_ref, back_lead_ref, middle_ref):
        pltpu.make_async_copy(target, target, one_sem.at[9]).wait()
    arrived(0, 0)
    for chunk in range(4):
        arrived(1, chunk)
        if chunk + AHEAD < 4:
            send_fields(1, chunk + AHEAD)
        convolve(2 * chunk)
        convolve(2 * chunk + 1)

    back = dot3(split(sum_ref[...]), table(back_trail_ref))
    real, imag = back[:, :128], back[:, 128:]
    cos, sin = twist_ref[0], twist_ref[1]
    turned = jnp.concatenate([real * cos + imag * sin, imag * cos - real * sin], axis=0)
    conv_ref[...] = dot3(table(back_lead_ref), split(turned)).reshape(16, 16, 128)

    def by_i(i):
        return at(z=i // 2, x=x // 2 * 2 + i % 2)

    def by_j(j):
        return at(y=j // 4, x=j % 4 // 2 * 2 + x % 2, core=j % 2)

    def exchange(source, target, to, own, sems):
        pltpu.make_async_copy(source.at[own], target.at[own], sems[1]).start()
        for o in range(1, 16):
            index = (own + o) % 16
            pltpu.make_async_remote_copy(
                src_ref=source.at[index],
                dst_ref=target.at[own],
                send_sem=sems[0],
                recv_sem=sems[1],
                device_id=device(to(index)),
                device_id_type=MESH,
            ).start()
        pltpu.make_async_copy(target, target, sems[1]).wait()

    exchange(conv_ref, got_ref.at[0], by_i, mine_i, (one_sem.at[18], one_sem.at[19]))
    values = [(got_ref[0, i, :8], got_ref[0, i, 8:]) for i in range(16)]
    for a, (real, imag) in enumerate(short_dft(values)):
        cos, sin = middle_ref[2 * a : 2 * a + 1], middle_ref[2 * a + 1 : 2 * a + 2]
        part_ref[a, :8] = real * cos - imag * sin
        part_ref[a, 8:] = real * sin + imag * cos
    exchange(part_ref, got_ref.at[1], by_j, mine_j, (one_sem.at[20], one_sem.at[21]))
    values = [(got_ref[1, i, :8], got_ref[1, i, 8:]) for i in range(16)]
    for a, value in enumerate(short_dft(values)):
        line_ref[a] = scaled(value, a, 64)[0]
    exchange(line_ref, out_ref, by_i, mine_i, (one_sem.at[22], one_sem.at[23]))

    for copy in started:
        copy.wait_send()
    for sent, sem in (
        (dense_ref.at[0, pl.ds(0, 8), 0], 1),
        (dense_ref.at[0, pl.ds(0, 3), 0], 2),
        (dense_ref.at[0, :, pl.ds(0, 3)], 32),
        (dense_ref.at[1, pl.ds(0, 8)], 34),
        (dense_ref.at[0, pl.ds(0, 7), 0], 36),
    ):
        await_block(sent, one_sem.at[sem])
    sent = field_ref.at[:, pl.ds(0, 7)]
    pltpu.make_async_copy(sent, sent, one_sem.at[5]).wait()
    for source, sem in ((conv_ref, 18), (part_ref, 20), (line_ref, 22)):
        sent = source.at[pl.ds(0, 15)]
        pltpu.make_async_copy(sent, sent, one_sem.at[sem]).wait()


def body(density, row_left, col_left, row_right, col_right):
    lines = density.reshape(4, 16, 8, 128).transpose(1, 2, 0, 3)
    constants = [jnp.asarray(c) for c in tables(256 * 16384)]
    vmem = pl.BlockSpec(memory_space=pltpu.VMEM)
    here = pl.BlockSpec(memory_space=pl.ANY)
    out = pl.pallas_call(
        kernel,
        out_shape=jax.ShapeDtypeStruct((16, 8, 128), F32),
        in_specs=[here, vmem, vmem] + [here] * 9,
        out_specs=here,
        scratch_shapes=[
            pltpu.VMEM((16, 4, 8, 128), F32),
            pltpu.VMEM((2, 16, 4, 4, 8, 128), F32),
            pltpu.VMEM((2, 2, 256, 256), BF16),
            pltpu.VMEM((2, 8, 8, 4, 8, 128), F32),
            pltpu.VMEM((16, 8, 4, 8, 128), F32),
            pltpu.VMEM((2, 16, 1024), F32),
            pltpu.VMEM((16, 2, 256), F32),
            pltpu.VMEM((2, 512, 256), BF16),
            pltpu.VMEM((2, 256, 128), F32),
            pltpu.VMEM((2, 256, 256), BF16),
            pltpu.VMEM((2, 256, 256), BF16),
            pltpu.VMEM((2, 256, 512), BF16),
            pltpu.VMEM((32, 128), F32),
            pltpu.VMEM((256, 256), F32),
            pltpu.VMEM((16, 16, 128), F32),
            pltpu.VMEM((2, 16, 16, 128), F32),
            pltpu.VMEM((16, 16, 128), F32),
            pltpu.VMEM((16, 8, 128), F32),
            pltpu.SemaphoreType.DMA((37,)),
            pltpu.SemaphoreType.DMA((16,)),
            pltpu.SemaphoreType.DMA((16,)),
            pltpu.SemaphoreType.REGULAR,
        ],
        compiler_params=pltpu.CompilerParams(
            collective_id=0, has_side_effects=True, vmem_limit_bytes=60 << 20
        ),
    )(lines, row_left, row_right, col_left, col_right, *constants)
    return out.reshape(1, 16384)


def solution(mesh):
    return jax.shard_map(
        body,
        mesh=mesh,
        in_specs=(P("comp", None), P(), P(), P(), P()),
        out_specs=P(("comp", "rank"), None),
        check_vma=False,
    )
```

```python
import functools
import math

import jax
import jax.numpy as jnp
import ml_dtypes
import numpy as np
from jax import lax
from jax.experimental import pallas as pl
from jax.experimental.pallas import tpu as pltpu
from jax.sharding import PartitionSpec as P

MESH = pl.DeviceIdType.MESH
BF16 = jnp.bfloat16
F32 = jnp.float32
SIZE = {"x": 4, "y": 4, "z": 8}


def halves(table):
    table = np.asarray(table, np.float64)
    high = table.astype(ml_dtypes.bfloat16)
    low = (table - high.astype(np.float64)).astype(ml_dtypes.bfloat16)
    return np.stack([high, low])


def phase(numerator, length, sign):
    angle = sign * 2.0 * np.pi * (np.asarray(numerator) % length) / length
    return np.cos(angle), np.sin(angle)


def as_real(cos, sin):
    return np.block([[cos, -sin], [sin, cos]])


def tables(total):
    k1, t1 = np.arange(256)[:, None], np.arange(128)[None, :]
    k2, s = np.arange(128)[:, None], np.arange(128)[None, :]
    a, k = np.arange(256)[None, :], np.arange(256)[:, None]
    turn = np.stack(phase(a * (4 * k + 1), 1024, -1), axis=1).astype(np.float32)
    lead = as_real(*phase(k1 * t1, 256, -1))
    twist = np.stack(phase(k1 * s, 32768, -1)).astype(np.float32)
    trail = as_real(*phase(k2 * s, 128, -1)).T
    back_trail = as_real(*phase(k2 * s, 128, 1)).T
    back_lead = as_real(*phase(np.arange(128)[:, None] * np.arange(256)[None, :], 256, 1))
    order = [8 * i + t + 128 * part for i in range(16) for part in (0, 1) for t in range(8)]
    back_lead = back_lead[np.array(order)]
    scale = 0.5 / (math.sqrt(total) * 256.0 * 32768.0)
    j, a0 = np.arange(16)[:, None], np.arange(16)[None, :]
    middle = scale * np.stack(phase(a0 * (4 * j + 1), 1024, 1), axis=2).reshape(16, 32, 1)
    middle = np.broadcast_to(middle, (16, 32, 128)).astype(np.float32)
    return turn, halves(lead), twist, halves(trail), halves(back_trail), halves(back_lead), middle


def scaled(value, numerator, length):
    real, imag = value
    cos, sin = (float(v) for v in phase(numerator, length, 1))
    if numerator == 0:
        return value
    if 4 * numerator == length:
        return -imag, real
    return real * cos - imag * sin, real * sin + imag * cos


def short_dft(values):
    length = len(values)
    if length == 1:
        return values
    even, odd = short_dft(values[0::2]), short_dft(values[1::2])
    odd = [scaled(v, n, length) for n, v in enumerate(odd)]
    pairs = list(zip(even, odd))
    return [(e[0] + o[0], e[1] + o[1]) for e, o in pairs] + [
        (e[0] - o[0], e[1] - o[1]) for e, o in pairs
    ]


def split(value):
    high = value.astype(BF16)
    return high, (value - high.astype(F32)).astype(BF16)


def dot3(first, second):
    dot = functools.partial(jnp.dot, preferred_element_type=F32)
    return dot(first[0], second[0]) + (dot(first[0], second[1]) + dot(first[1], second[0]))


def place():
    comp, rank = lax.axis_index("comp"), lax.axis_index("rank")
    return {"z": comp // 8, "y": comp % 4, "x": rank // 2 * 2 + comp // 4 % 2, "core": rank % 2}


def device(at):
    return {"comp": (at["z"] * 2 + at["x"] % 2) * 4 + at["y"], "rank": at["x"] // 2 * 2 + at["core"]}


def kernel(
    d_ref, row_left_ref, row_right_ref, left_ref, right_ref,
    turn_hbm, lead_hbm, twist_hbm, trail_hbm, back_trail_hbm, back_lead_hbm, middle_hbm,
    out_ref,
    lines_ref, dense_ref, weight_ref, field_ref, all_ref, cols_ref,
    turn_ref, lead_ref, twist_ref, trail_ref, back_trail_ref, back_lead_ref, middle_ref,
    sum_ref, conv_ref, got_ref, part_ref, line_ref,
    one_sem, recv_sem, pair_sem,
):
    me = place()
    z, y, x, core = me["z"], me["y"], me["x"], me["core"]
    mine = (z * 2 + x % 2, y)

    def at(**changes):
        moved = dict(me)
        for axis, value in changes.items():
            moved[axis] = value % SIZE[axis] if axis in SIZE else value
        return moved

    def group_x(where):
        return where["x"] % 2 * 4 + where["x"] // 2 * 2 + where["core"]

    def group_y(where):
        return where["y"] * 2 + where["core"]

    def group(region, where):
        return group_x(where) if region == 0 else group_y(where)

    def member(region, p):
        if region == 0:
            return at(x=p // 4 + p % 4 // 2 * 2, core=p % 2)
        return at(y=p // 2, core=p % 2)

    for row in range(4):
        pltpu.make_async_copy(d_ref.at[:, :, row], lines_ref.at[:, row], one_sem.at[0]).start()
    barrier = pltpu.get_barrier_semaphore()
    friends = [at(z=z + o) for o in (2, 6, 1, 7)]
    friends += [at(y=y + o) for o in range(1, 4)]
    friends += [at(x=x + o) for o in (1, 3)]
    friends += [at(core=1 - core)]
    for friend in friends:
        pl.semaphore_signal(barrier, inc=1, device_id=device(friend), device_id_type=MESH)

    for region in (0, 1):
        for p in range(8):
            owner = device(member(region, p))
            pltpu.make_async_copy(
                turn_hbm.at[4 * owner["comp"] + owner["rank"]],
                turn_ref.at[8 * region + p],
                one_sem.at[7],
            ).start()
    for region in (0, 1):
        columns = pl.ds(pl.multiple_of(1024 * (8 * region + group(region, me)), 1024), 1024)
        for side, source in enumerate((left_ref, right_ref)):
            pltpu.make_async_copy(
                source.at[:, columns], cols_ref.at[region, pl.ds(8 * side, 8)], one_sem.at[8]
            ).start()
    mine_j = y * 4 + x // 2 * 2 + core
    mine_i = z * 2 + x % 2
    for source, target in (
        (lead_hbm, lead_ref),
        (twist_hbm, twist_ref),
        (trail_hbm, trail_ref),
        (back_trail_hbm, back_trail_ref),
        (back_lead_hbm, back_lead_ref),
        (middle_hbm.at[mine_j], middle_ref),
    ):
        pltpu.make_async_copy(source, target, one_sem.at[9]).start()
    pltpu.make_async_copy(turn_ref, turn_ref, one_sem.at[7]).wait()
    both = jnp.concatenate([row_left_ref[...], row_right_ref[...]], axis=0)
    for region in (0, 1):
        for p in range(8):
            turn = turn_ref[8 * region + p]
            for part in (0, 1):
                high, low = split(both * turn[part : part + 1])
                first = 32 * p + 16 * part
                weight_ref[region, 0, first : first + 16] = high
                weight_ref[region, 1, first : first + 16] = low

    pltpu.make_async_copy(lines_ref, lines_ref, one_sem.at[0]).wait()
    pl.semaphore_wait(barrier, len(friends))

    def slices(region, where):
        return lines_ref.at[8 * region + group(region, where)]

    def copy(source, block, sender, receiver, target):
        pltpu.make_async_remote_copy(
            src_ref=source,
            dst_ref=block,
            send_sem=sender,
            recv_sem=receiver,
            device_id=device(target),
            device_id_type=MESH,
        ).start()

    def await_block(block, sem):
        pltpu.make_async_copy(block, block, sem).wait()

    first_block = dense_ref.at[(0,) + mine]
    second_block = dense_ref.at[(1,) + mine]
    beside = at(x=x - 1 + z % 2 * 2)
    copy(slices(0, beside), first_block, one_sem.at[1], one_sem.at[24], beside)
    for o in range(1, 4):
        target = at(y=y + o)
        copy(slices(1, target), second_block, one_sem.at[2], one_sem.at[4], target)
    own = pltpu.make_async_copy(slices(0, me), first_block, one_sem.at[3])
    own.start()
    pltpu.make_async_copy(slices(1, me), second_block, one_sem.at[4]).start()
    def block_z(o, half=None):
        index = (z + o) % 8 * 2 + x % 2
        if half is None:
            return dense_ref.at[1, index]
        return dense_ref.at[1, index, pl.ds(2 * half, 2)]

    def along_z(block, way, sem):
        copy(block, block, one_sem.at[37], recv_sem.at[sem], at(z=z + way))

    def along_y(o):
        block = dense_ref.at[0, pl.ds((z - o) % 8 * 2, 2), y]
        if o:
            await_block(block, one_sem.at[24 + o])
        for step in (2, 1, 3):
            copy(block, block, one_sem.at[32], one_sem.at[33], at(y=y + step))

    def along_x(o):
        index = (z + o) % 8
        block = block_z(o)
        copy(block, block, one_sem.at[34], one_sem.at[35], at(x=x + 1 - index % 2 * 2))

    def first_z(o):
        block = dense_ref.at[0, pl.ds(2 * z, 2), y]
        copy(block, block, one_sem.at[36], one_sem.at[24 + o], at(z=z + o))

    await_block(dense_ref.at[1, z * 2 + x % 2], one_sem.at[4])
    for sem, way in ((0, 2), (1, -2), (2, 1), (3, -1)):
        along_z(block_z(0), way, sem)
    along_x(0)
    await_block(dense_ref.at[0, z * 2 + 1 - x % 2, y], one_sem.at[24])
    own.wait()
    pl.semaphore_signal(
        pair_sem, inc=1, device_id=device(at(core=1 - core)), device_id_type=MESH
    )
    first_z(1)
    first_z(7)
    along_y(0)
    await_block(block_z(-2), recv_sem.at[0])
    along_z(block_z(-2), 1, 4)
    along_z(block_z(-2, 0), 2, 5)
    await_block(block_z(2), recv_sem.at[1])
    along_z(block_z(2), -1, 6)
    along_z(block_z(2, 1), -2, 7)
    first_z(2)
    first_z(6)
    await_block(block_z(-1), recv_sem.at[2])
    await_block(block_z(1), recv_sem.at[3])
    for o in (-1, 1, -2, 2):
        along_x(o)
    along_y(1)
    along_y(7)
    first_z(3)
    first_z(5)
    first_z(4)
    along_y(2)
    along_y(6)
    await_block(block_z(-3), recv_sem.at[4])
    along_x(-3)
    await_block(block_z(3), recv_sem.at[6])
    along_x(3)
    await_block(block_z(4, 0), recv_sem.at[5])
    await_block(block_z(4, 1), recv_sem.at[7])
    along_x(4)
    for o in (3, 5, 4):
        along_y(o)

    counts = (1, 1)

    def region_fields(region):
        weights = (weight_ref[region, 0], weight_ref[region, 1])
        source = dense_ref.at[region].reshape(256 * 8, 128)
        target = field_ref.at[region].reshape(256 * 8, 128)
        for t in range(0, 8, 2):
            pair = jnp.concatenate(
                [source[pl.ds(u, 256, stride=8), :] for u in (t, t + 1)], axis=1
            )
            field = dot3(weights, split(pair))
            cols = cols_ref[region, :, t * 128 : t * 128 + 256]
            field = (field.reshape(16, 16, 256) * cols[None]).reshape(256, 256)
            for u in (0, 1):
                lanes = slice(u * 128, u * 128 + 128)
                for p in range(8):
                    for kind in range(4):
                        low = 32 * p + 8 * kind
                        at_rows = pl.ds(256 * p + 8 * kind + t + u, 8, stride=32)
                        target[at_rows, :] = field[low : low + 8, lanes]

    def send_fields(region, chunk):
        own = group(region, me)
        terms = 8 // counts[region]
        which = pl.ds(terms * chunk, terms)
        landing = all_ref.at[8 * region + own, which]
        recv = one_sem.at[10 + 4 * region + chunk]
        pltpu.make_async_copy(field_ref.at[region, own, which], landing, recv).start()
        for o, c in [(2, 0), (2, 1), (1, 0), (3, 1), (1, 1), (3, 0), (0, 1)]:
            moved = {"core": (core + c) % 2, "xy"[region]: me["xy"[region]] + o}
            moved = at(**moved)
            source = field_ref.at[region, group(region, moved), which]
            copy(source, landing, one_sem.at[5], recv, moved)

    def arrived(region, chunk):
        terms = 8 // counts[region]
        block = all_ref.at[pl.ds(8 * region, 8), pl.ds(terms * chunk, terms)]
        pltpu.make_async_copy(block, block, one_sem.at[10 + 4 * region + chunk]).wait()

    def table(ref):
        return ref[0], ref[1]

    def convolve(r):
        x = jnp.concatenate(
            [
                jnp.concatenate([all_ref[:, r, 2 * part + side].reshape(128, 128) for side in (0, 1)], axis=1)
                for part in (0, 1)
            ],
            axis=0,
        )
        y = dot3(table(lead_ref), split(x))
        spectra = []
        for side in (0, 1):
            lanes = slice(side * 128, side * 128 + 128)
            real, imag = y[:256, lanes], y[256:, lanes]
            cos, sin = twist_ref[0], twist_ref[1]
            turned = jnp.concatenate([real * cos - imag * sin, real * sin + imag * cos], axis=1)
            spectra.append(dot3(split(turned), table(trail_ref)))
        left, right = spectra
        lr, li, rr, ri = left[:, :128], left[:, 128:], right[:, :128], right[:, 128:]
        sum_ref[:, :128] += lr * rr - li * ri
        sum_ref[:, 128:] += lr * ri + li * rr

    pltpu.make_async_copy(cols_ref, cols_ref, one_sem.at[8]).wait()
    await_block(dense_ref.at[0, :, pl.ds(0, 3)], one_sem.at[33])
    pl.semaphore_wait(pair_sem, 1)
    region_fields(0)
    send_fields(0, 0)
    await_block(dense_ref.at[1, pl.ds(0, 8)], one_sem.at[35])
    region_fields(1)
    send_fields(1, 0)
    sum_ref[...] = jnp.zeros_like(sum_ref)
    for target in (lead_ref, twist_ref, trail_ref, back_trail_ref, back_lead_ref, middle_ref):
        pltpu.make_async_copy(target, target, one_sem.at[9]).wait()
    arrived(0, 0)
    arrived(1, 0)
    for r in range(8):
        convolve(r)

    back = dot3(split(sum_ref[...]), table(back_trail_ref))
    real, imag = back[:, :128], back[:, 128:]
    cos, sin = twist_ref[0], twist_ref[1]
    turned = jnp.concatenate([real * cos + imag * sin, imag * cos - real * sin], axis=0)
    conv_ref[...] = dot3(table(back_lead_ref), split(turned)).reshape(16, 16, 128)

    def others_i():
        for dz in (4, 3, 5, 2, 6, 1, 7, 0):
            for dx in (1, 0):
                if dz or dx:
                    to = at(z=z + dz, x=x // 2 * 2 + (x + dx) % 2)
                    yield to["z"] * 2 + to["x"] % 2, to

    def others_j():
        for dy in (2, 1, 3, 0):
            for dx in (2, 0):
                for dc in (1, 0):
                    if dy or dx or dc:
                        to = at(y=y + dy, x=x + dx, core=(core + dc) % 2)
                        yield to["y"] * 4 + to["x"] // 2 * 2 + to["core"], to

    def exchange(source, target, others, own, sems):
        for index, to in others():
            copy(source.at[index], target.at[own], sems[0], sems[1], to)
        pltpu.make_async_copy(source.at[own], target.at[own], sems[1]).start()
        pltpu.make_async_copy(target, target, sems[1]).wait()

    exchange(conv_ref, got_ref.at[0], others_i, mine_i, (one_sem.at[18], one_sem.at[19]))
    values = [(got_ref[0, i, :8], got_ref[0, i, 8:]) for i in range(16)]
    for a, (real, imag) in enumerate(short_dft(values)):
        cos, sin = middle_ref[2 * a : 2 * a + 1], middle_ref[2 * a + 1 : 2 * a + 2]
        part_ref[a, :8] = real * cos - imag * sin
        part_ref[a, 8:] = real * sin + imag * cos
    exchange(part_ref, got_ref.at[1], others_j, mine_j, (one_sem.at[20], one_sem.at[21]))
    values = [(got_ref[1, i, :8], got_ref[1, i, 8:]) for i in range(16)]
    for a, value in enumerate(short_dft(values)):
        line_ref[a] = scaled(value, a, 64)[0]
    exchange(line_ref, out_ref, others_i, mine_i, (one_sem.at[22], one_sem.at[23]))

    for sent, sem in (
        (dense_ref.at[0, 0, 0], 1),
        (dense_ref.at[0, pl.ds(0, 3), 0], 2),
        (dense_ref.at[0, :, pl.ds(0, 3)], 32),
        (dense_ref.at[1, pl.ds(0, 8)], 34),
        (dense_ref.at[0, pl.ds(0, 14), 0], 36),
        (dense_ref.at[1, pl.ds(0, 7)], 37),
    ):
        await_block(sent, one_sem.at[sem])
    sent = field_ref.at[:, pl.ds(0, 7)]
    pltpu.make_async_copy(sent, sent, one_sem.at[5]).wait()
    for source, sem in ((conv_ref, 18), (part_ref, 20), (line_ref, 22)):
        sent = source.at[pl.ds(0, 15)]
        pltpu.make_async_copy(sent, sent, one_sem.at[sem]).wait()


def body(density, row_left, col_left, row_right, col_right):
    lines = density.reshape(4, 16, 8, 128).transpose(1, 2, 0, 3)
    constants = [jnp.asarray(c) for c in tables(256 * 16384)]
    vmem = pl.BlockSpec(memory_space=pltpu.VMEM)
    here = pl.BlockSpec(memory_space=pl.ANY)
    out = pl.pallas_call(
        kernel,
        out_shape=jax.ShapeDtypeStruct((16, 8, 128), F32),
        in_specs=[here, vmem, vmem] + [here] * 9,
        out_specs=vmem,
        scratch_shapes=[
            pltpu.VMEM((16, 4, 8, 128), F32),
            pltpu.VMEM((2, 16, 4, 4, 8, 128), F32),
            pltpu.VMEM((2, 2, 256, 256), BF16),
            pltpu.VMEM((2, 8, 8, 4, 8, 128), F32),
            pltpu.VMEM((16, 8, 4, 8, 128), F32),
            pltpu.VMEM((2, 16, 1024), F32),
            pltpu.VMEM((16, 2, 256), F32),
            pltpu.VMEM((2, 512, 256), BF16),
            pltpu.VMEM((2, 256, 128), F32),
            pltpu.VMEM((2, 256, 256), BF16),
            pltpu.VMEM((2, 256, 256), BF16),
            pltpu.VMEM((2, 256, 512), BF16),
            pltpu.VMEM((32, 128), F32),
            pltpu.VMEM((256, 256), F32),
            pltpu.VMEM((16, 16, 128), F32),
            pltpu.VMEM((2, 16, 16, 128), F32),
            pltpu.VMEM((16, 16, 128), F32),
            pltpu.VMEM((16, 8, 128), F32),
            pltpu.SemaphoreType.DMA((38,)),
            pltpu.SemaphoreType.DMA((8,)),
            pltpu.SemaphoreType.REGULAR,
        ],
        compiler_params=pltpu.CompilerParams(
            collective_id=0, has_side_effects=True, vmem_limit_bytes=55104 << 10
        ),
    )(lines, row_left, row_right, col_left, col_right, *constants)
    return out.reshape(1, 16384)


def solution(mesh):
    return jax.shard_map(
        body,
        mesh=mesh,
        in_specs=(P("comp", None), P(), P(), P(), P()),
        out_specs=P(("comp", "rank"), None),
        check_vma=False,
    )
```

```python
import functools
import math

import jax
import jax.numpy as jnp
import ml_dtypes
import numpy as np
from jax import lax
from jax.experimental import pallas as pl
from jax.experimental.pallas import tpu as pltpu
from jax.sharding import PartitionSpec as P

MESH = pl.DeviceIdType.MESH
BF16 = jnp.bfloat16
F32 = jnp.float32
SIZE = {"x": 4, "y": 4, "z": 8}


def halves(table):
    table = np.asarray(table, np.float64)
    high = table.astype(ml_dtypes.bfloat16)
    low = (table - high.astype(np.float64)).astype(ml_dtypes.bfloat16)
    return np.stack([high, low])


def phase(numerator, length, sign):
    angle = sign * 2.0 * np.pi * (np.asarray(numerator) % length) / length
    return np.cos(angle), np.sin(angle)


def as_real(cos, sin):
    return np.block([[cos, -sin], [sin, cos]])


def tables(total):
    k1, t1 = np.arange(256)[:, None], np.arange(128)[None, :]
    k2, s = np.arange(128)[:, None], np.arange(128)[None, :]
    a, k = np.arange(256)[None, :], np.arange(256)[:, None]
    turn = np.stack(phase(a * (4 * k + 1), 1024, -1), axis=1).astype(np.float32)
    lead = as_real(*phase(k1 * t1, 256, -1))
    twist = np.stack(phase(k1 * s, 32768, -1)).astype(np.float32)
    trail = as_real(*phase(k2 * s, 128, -1)).T
    back_trail = as_real(*phase(k2 * s, 128, 1)).T
    back_lead = as_real(*phase(np.arange(128)[:, None] * np.arange(256)[None, :], 256, 1))
    order = [8 * i + t + 128 * part for i in range(16) for part in (0, 1) for t in range(8)]
    back_lead = back_lead[np.array(order)]
    scale = 0.5 / (math.sqrt(total) * 256.0 * 32768.0)
    j, a0 = np.arange(16)[:, None], np.arange(16)[None, :]
    middle = scale * np.stack(phase(a0 * (4 * j + 1), 1024, 1), axis=2).reshape(16, 32, 1)
    middle = np.broadcast_to(middle, (16, 32, 128)).astype(np.float32)
    return turn, halves(lead), twist, halves(trail), halves(back_trail), halves(back_lead), middle


def scaled(value, numerator, length):
    real, imag = value
    cos, sin = (float(v) for v in phase(numerator, length, 1))
    if numerator == 0:
        return value
    if 4 * numerator == length:
        return -imag, real
    return real * cos - imag * sin, real * sin + imag * cos


def short_dft(values):
    length = len(values)
    if length == 1:
        return values
    even, odd = short_dft(values[0::2]), short_dft(values[1::2])
    odd = [scaled(v, n, length) for n, v in enumerate(odd)]
    pairs = list(zip(even, odd))
    return [(e[0] + o[0], e[1] + o[1]) for e, o in pairs] + [
        (e[0] - o[0], e[1] - o[1]) for e, o in pairs
    ]


def split(value):
    high = value.astype(BF16)
    return high, (value - high.astype(F32)).astype(BF16)


def dot3(first, second):
    dot = functools.partial(jnp.dot, preferred_element_type=F32)
    return dot(first[0], second[0]) + (dot(first[0], second[1]) + dot(first[1], second[0]))


def place():
    comp, rank = lax.axis_index("comp"), lax.axis_index("rank")
    return {"z": comp // 8, "y": comp % 4, "x": rank // 2 * 2 + comp // 4 % 2, "core": rank % 2}


def device(at):
    return {"comp": (at["z"] * 2 + at["x"] % 2) * 4 + at["y"], "rank": at["x"] // 2 * 2 + at["core"]}


def kernel(
    d_ref, row_left_ref, row_right_ref, left_ref, right_ref,
    turn_hbm, lead_hbm, twist_hbm, trail_hbm, back_trail_hbm, back_lead_hbm, middle_hbm,
    out_ref,
    lines_ref, dense_ref, weight_ref, field_ref, all_ref, cols_ref,
    turn_ref, lead_ref, twist_ref, trail_ref, back_trail_ref, back_lead_ref, middle_ref,
    sum_ref, conv_ref, got_ref, part_ref, line_ref,
    one_sem, recv_sem, pair_sem,
):
    me = place()
    z, y, x, core = me["z"], me["y"], me["x"], me["core"]
    mine = (z * 2 + x % 2, y)

    def at(**changes):
        moved = dict(me)
        for axis, value in changes.items():
            moved[axis] = value % SIZE[axis] if axis in SIZE else value
        return moved

    def group_x(where):
        return where["x"] % 2 * 4 + where["x"] // 2 * 2 + where["core"]

    def group_y(where):
        return where["y"] * 2 + where["core"]

    def group(region, where):
        return group_x(where) if region == 0 else group_y(where)

    def member(region, p):
        if region == 0:
            return at(x=p // 4 + p % 4 // 2 * 2, core=p % 2)
        return at(y=p // 2, core=p % 2)

    for row in range(4):
        pltpu.make_async_copy(d_ref.at[:, :, row], lines_ref.at[:, row], one_sem.at[0]).start()
    barrier = pltpu.get_barrier_semaphore()
    friends = [at(z=z + o) for o in (2, 6, 1, 7)]
    friends += [at(y=y + o) for o in range(1, 4)]
    friends += [at(x=x + o) for o in (1, 3)]
    friends += [at(core=1 - core)]
    for friend in friends:
        pl.semaphore_signal(barrier, inc=1, device_id=device(friend), device_id_type=MESH)

    for region in (0, 1):
        for p in range(8):
            owner = device(member(region, p))
            pltpu.make_async_copy(
                turn_hbm.at[4 * owner["comp"] + owner["rank"]],
                turn_ref.at[8 * region + p],
                one_sem.at[7],
            ).start()
    for region in (0, 1):
        columns = pl.ds(pl.multiple_of(1024 * (8 * region + group(region, me)), 1024), 1024)
        for side, source in enumerate((left_ref, right_ref)):
            pltpu.make_async_copy(
                source.at[:, columns], cols_ref.at[region, pl.ds(8 * side, 8)], one_sem.at[8]
            ).start()
    mine_j = y * 4 + x // 2 * 2 + core
    mine_i = z * 2 + x % 2
    for source, target in (
        (lead_hbm, lead_ref),
        (twist_hbm, twist_ref),
        (trail_hbm, trail_ref),
        (back_trail_hbm, back_trail_ref),
        (back_lead_hbm, back_lead_ref),
        (middle_hbm.at[mine_j], middle_ref),
    ):
        pltpu.make_async_copy(source, target, one_sem.at[9]).start()
    pltpu.make_async_copy(turn_ref, turn_ref, one_sem.at[7]).wait()
    both = jnp.concatenate([row_left_ref[...], row_right_ref[...]], axis=0)
    for region in (0, 1):
        for p in range(8):
            turn = turn_ref[8 * region + p]
            for part in (0, 1):
                high, low = split(both * turn[part : part + 1])
                first = 32 * p + 16 * part
                weight_ref[region, 0, first : first + 16] = high
                weight_ref[region, 1, first : first + 16] = low

    pltpu.make_async_copy(lines_ref, lines_ref, one_sem.at[0]).wait()
    pl.semaphore_wait(barrier, len(friends))

    def slices(region, where):
        return lines_ref.at[8 * region + group(region, where)]

    def copy(source, block, sender, receiver, target):
        pltpu.make_async_remote_copy(
            src_ref=source,
            dst_ref=block,
            send_sem=sender,
            recv_sem=receiver,
            device_id=device(target),
            device_id_type=MESH,
        ).start()

    def await_block(block, sem):
        pltpu.make_async_copy(block, block, sem).wait()

    first_block = dense_ref.at[(0,) + mine]
    second_block = dense_ref.at[(1,) + mine]
    beside = at(x=x - 1 + z % 2 * 2)
    copy(slices(0, beside), first_block, one_sem.at[1], one_sem.at[24], beside)
    for o in range(1, 4):
        target = at(y=y + o)
        copy(slices(1, target), second_block, one_sem.at[2], one_sem.at[4], target)
    own = pltpu.make_async_copy(slices(0, me), first_block, one_sem.at[3])
    own.start()
    pltpu.make_async_copy(slices(1, me), second_block, one_sem.at[4]).start()
    def block_z(o, half=None):
        index = (z + o) % 8 * 2 + x % 2
        if half is None:
            return dense_ref.at[1, index]
        return dense_ref.at[1, index, pl.ds(2 * half, 2)]

    def along_z(block, way, sem):
        copy(block, block, one_sem.at[37], recv_sem.at[sem], at(z=z + way))

    def along_y(o):
        block = dense_ref.at[0, pl.ds((z - o) % 8 * 2, 2), y]
        if o:
            await_block(block, one_sem.at[24 + o])
        for step in (2, 1, 3):
            copy(block, block, one_sem.at[32], one_sem.at[33], at(y=y + step))

    def along_x(o):
        index = (z + o) % 8
        block = block_z(o)
        copy(block, block, one_sem.at[34], one_sem.at[35], at(x=x + 1 - index % 2 * 2))

    def first_z(o):
        block = dense_ref.at[0, pl.ds(2 * z, 2), y]
        copy(block, block, one_sem.at[36], one_sem.at[24 + o], at(z=z + o))

    await_block(dense_ref.at[1, z * 2 + x % 2], one_sem.at[4])
    for sem, way in ((0, 2), (1, -2), (2, 1), (3, -1)):
        along_z(block_z(0), way, sem)
    along_x(0)
    await_block(dense_ref.at[0, z * 2 + 1 - x % 2, y], one_sem.at[24])
    own.wait()
    pl.semaphore_signal(
        pair_sem, inc=1, device_id=device(at(core=1 - core)), device_id_type=MESH
    )
    first_z(1)
    first_z(7)
    along_y(0)
    await_block(block_z(-2), recv_sem.at[0])
    along_z(block_z(-2), 1, 4)
    along_z(block_z(-2, 0), 2, 5)
    await_block(block_z(2), recv_sem.at[1])
    along_z(block_z(2), -1, 6)
    along_z(block_z(2, 1), -2, 7)
    first_z(2)
    first_z(6)
    await_block(block_z(-1), recv_sem.at[2])
    await_block(block_z(1), recv_sem.at[3])
    for o in (-1, 1, -2, 2):
        along_x(o)
    along_y(1)
    along_y(7)
    first_z(3)
    first_z(5)
    first_z(4)
    along_y(2)
    along_y(6)
    await_block(block_z(-3), recv_sem.at[4])
    along_x(-3)
    await_block(block_z(3), recv_sem.at[6])
    along_x(3)
    await_block(block_z(4, 0), recv_sem.at[5])
    await_block(block_z(4, 1), recv_sem.at[7])
    along_x(4)
    for o in (3, 5, 4):
        along_y(o)

    counts = (1, 1)

    def region_fields(region):
        weights = (weight_ref[region, 0], weight_ref[region, 1])
        source = dense_ref.at[region].reshape(256 * 8, 128)
        target = field_ref.at[region].reshape(256 * 8, 128)
        for t in range(0, 8, 2):
            pair = jnp.concatenate(
                [source[pl.ds(u, 256, stride=8), :] for u in (t, t + 1)], axis=1
            )
            field = dot3(weights, split(pair))
            cols = cols_ref[region, :, t * 128 : t * 128 + 256]
            field = (field.reshape(16, 16, 256) * cols[None]).reshape(256, 256)
            for u in (0, 1):
                lanes = slice(u * 128, u * 128 + 128)
                for p in range(8):
                    for kind in range(4):
                        low = 32 * p + 8 * kind
                        at_rows = pl.ds(256 * p + 8 * kind + t + u, 8, stride=32)
                        target[at_rows, :] = field[low : low + 8, lanes]

    def send_fields(region, chunk):
        own = group(region, me)
        terms = 8 // counts[region]
        which = pl.ds(terms * chunk, terms)
        landing = all_ref.at[8 * region + own, which]
        recv = one_sem.at[10 + 4 * region + chunk]
        pltpu.make_async_copy(field_ref.at[region, own, which], landing, recv).start()
        for o, c in [(2, 0), (2, 1), (1, 0), (3, 1), (1, 1), (3, 0), (0, 1)]:
            moved = {"core": (core + c) % 2, "xy"[region]: me["xy"[region]] + o}
            moved = at(**moved)
            source = field_ref.at[region, group(region, moved), which]
            copy(source, landing, one_sem.at[5], recv, moved)

    def arrived(region, chunk):
        terms = 8 // counts[region]
        block = all_ref.at[pl.ds(8 * region, 8), pl.ds(terms * chunk, terms)]
        pltpu.make_async_copy(block, block, one_sem.at[10 + 4 * region + chunk]).wait()

    def table(ref):
        return ref[0], ref[1]

    def convolve(r):
        x = jnp.concatenate(
            [
                jnp.concatenate([all_ref[:, r, 2 * part + side].reshape(128, 128) for side in (0, 1)], axis=1)
                for part in (0, 1)
            ],
            axis=0,
        )
        y = dot3(table(lead_ref), split(x))
        spectra = []
        for side in (0, 1):
            lanes = slice(side * 128, side * 128 + 128)
            real, imag = y[:256, lanes], y[256:, lanes]
            cos, sin = twist_ref[0], twist_ref[1]
            turned = jnp.concatenate([real * cos - imag * sin, real * sin + imag * cos], axis=1)
            spectra.append(dot3(split(turned), table(trail_ref)))
        left, right = spectra
        lr, li, rr, ri = left[:, :128], left[:, 128:], right[:, :128], right[:, 128:]
        sum_ref[:, :128] += lr * rr - li * ri
        sum_ref[:, 128:] += lr * ri + li * rr

    pltpu.make_async_copy(cols_ref, cols_ref, one_sem.at[8]).wait()
    await_block(dense_ref.at[1, pl.ds(0, 8)], one_sem.at[35])
    pl.semaphore_wait(pair_sem, 1)
    region_fields(1)
    send_fields(1, 0)
    await_block(dense_ref.at[0, :, pl.ds(0, 3)], one_sem.at[33])
    region_fields(0)
    send_fields(0, 0)
    sum_ref[...] = jnp.zeros_like(sum_ref)
    for target in (lead_ref, twist_ref, trail_ref, back_trail_ref, back_lead_ref, middle_ref):
        pltpu.make_async_copy(target, target, one_sem.at[9]).wait()
    arrived(0, 0)
    arrived(1, 0)
    for r in range(8):
        convolve(r)

    back = dot3(split(sum_ref[...]), table(back_trail_ref))
    real, imag = back[:, :128], back[:, 128:]
    cos, sin = twist_ref[0], twist_ref[1]
    turned = jnp.concatenate([real * cos + imag * sin, imag * cos - real * sin], axis=0)
    conv_ref[...] = dot3(table(back_lead_ref), split(turned)).reshape(16, 16, 128)

    def others_i():
        for dz in (4, 3, 5, 2, 6, 1, 7, 0):
            for dx in (1, 0):
                if dz or dx:
                    to = at(z=z + dz, x=x // 2 * 2 + (x + dx) % 2)
                    yield to["z"] * 2 + to["x"] % 2, to

    def others_j():
        for dy in (2, 1, 3, 0):
            for dx in (2, 0):
                for dc in (1, 0):
                    if dy or dx or dc:
                        to = at(y=y + dy, x=x + dx, core=(core + dc) % 2)
                        yield to["y"] * 4 + to["x"] // 2 * 2 + to["core"], to

    def exchange(source, target, others, own, sems):
        for index, to in others():
            copy(source.at[index], target.at[own], sems[0], sems[1], to)
        pltpu.make_async_copy(source.at[own], target.at[own], sems[1]).start()
        pltpu.make_async_copy(target, target, sems[1]).wait()

    exchange(conv_ref, got_ref.at[0], others_i, mine_i, (one_sem.at[18], one_sem.at[19]))
    values = [(got_ref[0, i, :8], got_ref[0, i, 8:]) for i in range(16)]
    for a, (real, imag) in enumerate(short_dft(values)):
        cos, sin = middle_ref[2 * a : 2 * a + 1], middle_ref[2 * a + 1 : 2 * a + 2]
        part_ref[a, :8] = real * cos - imag * sin
        part_ref[a, 8:] = real * sin + imag * cos
    exchange(part_ref, got_ref.at[1], others_j, mine_j, (one_sem.at[20], one_sem.at[21]))
    values = [(got_ref[1, i, :8], got_ref[1, i, 8:]) for i in range(16)]
    for a, value in enumerate(short_dft(values)):
        line_ref[a] = scaled(value, a, 64)[0]
    exchange(line_ref, out_ref, others_i, mine_i, (one_sem.at[22], one_sem.at[23]))

    for sent, sem in (
        (dense_ref.at[0, 0, 0], 1),
        (dense_ref.at[0, pl.ds(0, 3), 0], 2),
        (dense_ref.at[0, :, pl.ds(0, 3)], 32),
        (dense_ref.at[1, pl.ds(0, 8)], 34),
        (dense_ref.at[0, pl.ds(0, 14), 0], 36),
        (dense_ref.at[1, pl.ds(0, 7)], 37),
    ):
        await_block(sent, one_sem.at[sem])
    sent = field_ref.at[:, pl.ds(0, 7)]
    pltpu.make_async_copy(sent, sent, one_sem.at[5]).wait()
    for source, sem in ((conv_ref, 18), (part_ref, 20), (line_ref, 22)):
        sent = source.at[pl.ds(0, 15)]
        pltpu.make_async_copy(sent, sent, one_sem.at[sem]).wait()


def body(density, row_left, col_left, row_right, col_right):
    lines = density.reshape(4, 16, 8, 128).transpose(1, 2, 0, 3)
    constants = [jnp.asarray(c) for c in tables(256 * 16384)]
    vmem = pl.BlockSpec(memory_space=pltpu.VMEM)
    here = pl.BlockSpec(memory_space=pl.ANY)
    out = pl.pallas_call(
        kernel,
        out_shape=jax.ShapeDtypeStruct((16, 8, 128), F32),
        in_specs=[here, vmem, vmem] + [here] * 9,
        out_specs=vmem,
        scratch_shapes=[
            pltpu.VMEM((16, 4, 8, 128), F32),
            pltpu.VMEM((2, 16, 4, 4, 8, 128), F32),
            pltpu.VMEM((2, 2, 256, 256), BF16),
            pltpu.VMEM((2, 8, 8, 4, 8, 128), F32),
            pltpu.VMEM((16, 8, 4, 8, 128), F32),
            pltpu.VMEM((2, 16, 1024), F32),
            pltpu.VMEM((16, 2, 256), F32),
            pltpu.VMEM((2, 512, 256), BF16),
            pltpu.VMEM((2, 256, 128), F32),
            pltpu.VMEM((2, 256, 256), BF16),
            pltpu.VMEM((2, 256, 256), BF16),
            pltpu.VMEM((2, 256, 512), BF16),
            pltpu.VMEM((32, 128), F32),
            pltpu.VMEM((256, 256), F32),
            pltpu.VMEM((16, 16, 128), F32),
            pltpu.VMEM((2, 16, 16, 128), F32),
            pltpu.VMEM((16, 16, 128), F32),
            pltpu.VMEM((16, 8, 128), F32),
            pltpu.SemaphoreType.DMA((38,)),
            pltpu.SemaphoreType.DMA((8,)),
            pltpu.SemaphoreType.REGULAR,
        ],
        compiler_params=pltpu.CompilerParams(
            collective_id=0, has_side_effects=True, vmem_limit_bytes=55104 << 10
        ),
    )(lines, row_left, row_right, col_left, col_right, *constants)
    return out.reshape(1, 16384)


def solution(mesh):
    return jax.shard_map(
        body,
        mesh=mesh,
        in_specs=(P("comp", None), P(), P(), P(), P()),
        out_specs=P(("comp", "rank"), None),
        check_vma=False,
    )
```
